32 devices in a mesh: groups: 2 (over y), rows: 4 (over z), cols: 2 (over x), sub: 2 (over core).
Axes of the slice: x: 2, y: 2, z: 4, core: 2. Of those that a mesh axis runs over, the one named last changes fastest.
Arguments:
- displace: float32 [6, 65536], P(None, ('groups', 'rows', 'cols', 'sub')), parts along dimension 1, may hold values from -6 to 6
- velocity: float32 [6, 65536], P(None, ('groups', 'rows', 'cols', 'sub')), parts along dimension 1, may hold values from -6 to 6
- nodal_mass: float32 [65536], P(('groups', 'rows', 'cols', 'sub')), parts along dimension 0, may hold values from 0.5 to 2
- send_list: int32 [12, 6, 1024], P('rows', 'cols', ('groups', 'sub')), parts along dimension 2, may hold values from 0 to 2047
- beam_slots: int32 [6, 65536], P(None, ('groups', 'rows', 'cols', 'sub')), parts along dimension 1, may hold values from 0 to 8703, as said below
- shape_values: float32 [6, 65536], P(None, ('groups', 'rows', 'cols', 'sub')), parts along dimension 1, as said below
- beam_kind: int32 [65536], P(('groups', 'rows', 'cols', 'sub')), parts along dimension 0, may hold values from 0 to 7
- cluster_weight: float32 [65536], P(('groups', 'rows', 'cols', 'sub')), parts along dimension 0, may hold values from 0.5 to 5
- stiffness: float32 [8, 12, 12], replicated, may hold values from -1.75 to 1.75
Outputs:
- field_out: float32 [6, 65536], P(None, ('groups', 'rows', 'cols', 'sub')), parts along dimension 1
- velocity_out: float32 [6, 65536], P(None, ('groups', 'rows', 'cols', 'sub')), parts along dimension 1
The draws below stay inside these ranges and needn't reach their ends.
There are 2 independent parts, one for each index of `groups`. The reference program is written for one: setup_inputs(seed, part) draws one part's arguments, and reference() takes and returns one part's arrays. A program takes and returns all parts, laid end to end along the dimension named above; an argument that names none is the same for every part. Nothing has to cross between parts.
Inputs may be any that keep to these rules, and one draw needn't show every extreme that they name: `beam_slots`: below 2 * 2048 a slot is a repnode of the device's own block; above it the slot lies in a received list, never in list (1, 1). `shape_values`: Positive; the three values of each beam end sum to one.
All inputs are finite; a program needn't handle non-finite values.
Results may differ from the reference program's by a relative error of at most 0.0003.
Values sent between devices are 32-bit elements; how exact they have to be, the bound alone decides.
No kernel may reach another device: no remote copies, remote signals or barrier semaphores. Data moves between devices by JAX's collectives and lax.ppermute only.
A program may use at most 64 MiB of HBM per device.

```python
import math
import jax
import jax.numpy as jnp
from jax import lax

REP_DEV = 2048
CAP = 256
BEAMS = 2048
KINDS = 8
STEPS = 2
NREP = 32768
BEAMS_ALL = 32768
N_ROWS = 4
N_COLS = 2
N_SUB = 2


def draw_beam_slots(key, part):
    key = jax.random.fold_in(key, 11)
    local_count = N_SUB * REP_DEV
    picks = jax.random.randint(key, (6, BEAMS_ALL), 0, local_count + N_SUB * 8 * CAP, dtype=jnp.int32)
    offset = picks - local_count
    sender = offset // (8 * CAP)
    remain = offset % (8 * CAP)
    direction = remain // CAP
    position = remain % CAP
    direction = direction + (direction >= 4).astype(jnp.int32)
    slot = local_count + (sender * 9 + direction) * CAP + position
    return jnp.where(picks < local_count, picks, slot).astype(jnp.int32)


def draw_shape_values(key, part):
    key = jax.random.fold_in(key, 12)
    raw = jax.random.uniform(key, (2, 3, BEAMS_ALL), jnp.float32, 0.1, 1.0)
    values = raw / jnp.sum(raw, axis=1, keepdims=True)
    return values.reshape(6, BEAMS_ALL).astype(jnp.float32)


def touch_ends(array, stream_key, least, high):
    longest = array.shape.index(max(array.shape))
    spots = []
    for shift in (0, 1):
        where = [jax.random.randint(jax.random.fold_in(stream_key, axis), (), 0, length) for axis, length in enumerate(array.shape)]
        where[longest] = (where[longest] + shift) % array.shape[longest]
        spots.append(tuple(where))
    return array.at[spots[0]].set(least).at[spots[1]].set(high)


def levels(key, dims, shards, low, largest):
    def one(axis_at, parts):
        heights = jax.random.uniform(jax.random.fold_in(jax.random.fold_in(key, 6), axis_at), (parts,), jnp.float32, low / len(shards), largest / len(shards))
        return jnp.repeat(jnp.exp(heights), dims[axis_at] // parts).reshape((-1,) + (1,) * (len(dims) - axis_at - 1))

    gain = one(*shards[0])
    for cut in shards[1:]:
        gain = gain * one(*cut)
    return gain


def normal_values(rng, shape, spread, most, cuts=(), kind=jnp.bfloat16):
    level = levels(rng, shape, cuts, -0.22, 0.18) if cuts else 1.0
    entries = jax.random.normal(rng, shape, jnp.float32) * spread * level
    return jnp.minimum(jnp.maximum(entries, -most), most).astype(kind)


def setup_inputs(seed: int = 0, part: int = 0) -> dict:
    keys = jax.random.split(jax.random.key(seed), 10)
    own_keys = jax.random.split(jax.random.fold_in(keys[9], part), 10)
    return {
        "displace": normal_values(own_keys[0], (6, NREP), 1.0, 6.0, ((1, 16),), jnp.float32),
        "velocity": normal_values(own_keys[1], (6, NREP), 1.0, 6.0, ((1, 16),), jnp.float32),
        "nodal_mass": jnp.clip(jnp.exp(math.log(2.0) - 1.3862944 * jax.random.uniform(own_keys[2], (NREP,), jnp.float32) ** levels(own_keys[2], (NREP,), ((0, 16),), -0.2, 0.2)), 0.5, 2.0),
        "send_list": touch_ends(jax.random.randint(own_keys[3], (3 * N_ROWS, 3 * N_COLS, CAP * N_SUB), 0, REP_DEV), jax.random.fold_in(own_keys[3], 1), 0, REP_DEV - 1).astype(jnp.int32),
        "beam_slots": draw_beam_slots(jax.random.fold_in(jax.random.fold_in(keys[9], part), 71), part),
        "shape_values": draw_shape_values(jax.random.fold_in(jax.random.fold_in(keys[9], part), 71), part),
        "beam_kind": touch_ends(jax.random.randint(own_keys[6], (BEAMS_ALL,), 0, KINDS), jax.random.fold_in(own_keys[6], 1), 0, KINDS - 1).astype(jnp.int32),
        "cluster_weight": jnp.clip(jnp.exp(math.log(5.0) - 2.3025851 * jax.random.uniform(own_keys[7], (BEAMS_ALL,), jnp.float32) ** levels(own_keys[7], (BEAMS_ALL,), ((0, 16),), -0.2, 0.2)), 0.5, 5.0),
        "stiffness": normal_values(keys[8], (KINDS, 12, 12), 12 ** -0.5, 1.75, (), jnp.float32),
    }


def beam_forces(buffer, slot_pick, shape_pick, kind_pick, weight, stiffness):
    beam_count = slot_pick.shape[1]
    gathered = jnp.take(buffer, slot_pick, axis=1) * shape_pick[None]
    beam_ends = gathered.reshape(6, 2, 3, beam_count).sum(axis=2)
    beam_vec = beam_ends.transpose(1, 0, 2).reshape(12, beam_count)
    per_kind = jnp.einsum("tij,jb->tib", stiffness, beam_vec, precision=lax.Precision.HIGHEST)
    selector = (kind_pick[None, :] == jnp.arange(stiffness.shape[0], dtype=jnp.int32)[:, None]).astype(jnp.float32)
    beam_force = jnp.sum(per_kind * selector[:, None, :], axis=0)
    end_force = beam_force.reshape(2, 6, beam_count).transpose(1, 0, 2)
    scaled = shape_pick.reshape(2, 3, beam_count) * weight[None, None, :]
    per_slot = end_force[:, :, None, :] * scaled[None]
    contrib = jnp.zeros((6, buffer.shape[1]), jnp.float32)
    return contrib.at[:, slot_pick.reshape(-1)].add(per_slot.reshape(6, -1))


def reference(displace, velocity, nodal_mass, send_list, beam_slots, shape_values, beam_kind, cluster_weight, stiffness):
    R, C, S = N_ROWS, N_COLS, N_SUB
    D = R * C * S
    field_now = displace.reshape(6, D, REP_DEV).transpose(1, 0, 2)
    velocity_now = velocity.reshape(6, D, REP_DEV).transpose(1, 0, 2)
    masses = nodal_mass.reshape(D, 1, REP_DEV)
    send_rows = send_list.reshape(R, 3, C, 3, S, CAP).transpose(0, 2, 4, 1, 3, 5).reshape(D, 9 * CAP)
    slot_all = beam_slots.reshape(6, D, BEAMS).transpose(1, 0, 2)
    shape_all = shape_values.reshape(6, D, BEAMS).transpose(1, 0, 2)
    kind_all = beam_kind.reshape(D, BEAMS)
    weight_all = cluster_weight.reshape(D, BEAMS)
    blocks = jnp.arange(D, dtype=jnp.int32) // S
    for _ in range(STEPS):
        outgoing = jax.vmap(lambda piece, picks: jnp.take(piece, picks, axis=1))(field_now, send_rows)
        outgoing = outgoing.reshape(R, C, S, 6, 3, 3, CAP)
        padded = jnp.pad(outgoing, ((1, 1), (1, 1), (0, 0), (0, 0), (0, 0), (0, 0), (0, 0)))
        row_stacks = []
        for a in range(3):
            col_pieces = [padded[2 - a:2 - a + R, 2 - b:2 - b + C, :, :, a, b, :] for b in range(3)]
            row_stacks.append(jnp.stack(col_pieces, axis=3))
        arrived = jnp.stack(row_stacks, axis=3)
        near_part = arrived.transpose(0, 1, 5, 2, 3, 4, 6).reshape(R * C, 6, S * 9 * CAP)
        local_part = field_now.reshape(R, C, S, 6, REP_DEV).transpose(0, 1, 3, 2, 4).reshape(R * C, 6, S * REP_DEV)
        buffers = jnp.concatenate([local_part, near_part], axis=2)

        def one_device(inputs):
            block_id, slot_pick, shape_pick, kind_pick, weight = inputs
            return beam_forces(buffers[block_id], slot_pick, shape_pick, kind_pick, weight, stiffness)

        contrib = lax.map(one_device, (blocks, slot_all, shape_all, kind_all, weight_all))
        summed = contrib.reshape(R, C, S, 6, -1).sum(axis=2)
        own_force = summed[..., :S * REP_DEV].reshape(R, C, 6, S, REP_DEV).transpose(0, 1, 3, 2, 4).reshape(D, 6, REP_DEV)
        near_force = summed[..., S * REP_DEV:].reshape(R, C, 6, S, 3, 3, CAP).transpose(0, 1, 3, 4, 5, 2, 6)
        back_pad = jnp.pad(near_force, ((1, 1), (1, 1), (0, 0), (0, 0), (0, 0), (0, 0), (0, 0)))
        back_rows = []
        for a in range(3):
            col_pieces = [back_pad[a:a + R, b:b + C, :, a, b, :, :] for b in range(3)]
            back_rows.append(jnp.stack(col_pieces, axis=3))
        returned = jnp.stack(back_rows, axis=3).reshape(D, 3, 3, 6, CAP).transpose(0, 3, 1, 2, 4).reshape(D, 6, 9 * CAP)
        net_force = jax.vmap(lambda total, picks, values: total.at[:, picks].add(values))(own_force, send_rows, returned)
        velocity_now = 0.98 * velocity_now - 0.2 * net_force / masses
        field_now = field_now + 0.2 * velocity_now
    field_out = field_now.transpose(1, 0, 2).reshape(6, D * REP_DEV)
    velocity_out = velocity_now.transpose(1, 0, 2).reshape(6, D * REP_DEV)
    return (field_out, velocity_out)
```

```python
import functools

import jax
import jax.numpy as jnp
from jax import lax
from jax.experimental import pallas as pl
from jax.experimental.pallas import tpu as pltpu
from jax.sharding import PartitionSpec as P

STEPS = 2
F32 = jnp.float32
BF16 = jnp.bfloat16
VMEM = pl.BlockSpec(memory_space=pltpu.VMEM)


def lane_pick(row, lanes):
    return jnp.take_along_axis(row, lanes, axis=1, mode="promise_in_bounds")


def spread(row):
    return jnp.broadcast_to(row, (8, 128))


def pick_lists(field, picks_ref, outs):
    picks = [picks_ref[0:8, :], picks_ref[8:16, :]]
    lanes = [p & 127 for p in picks]
    rows = [lax.shift_right_logical(p, 7) for p in picks]
    found = [[jnp.zeros((8, 128), F32) for _ in range(2)] for _ in range(6)]
    for k in range(8):
        for half in range(2):
            hit = [r == 2 * k + half for r in rows]
            for c in range(6):
                row = spread(field[2 * c + half, k : k + 1, :])
                for v in range(2):
                    found[c][v] = jnp.where(hit[v], lane_pick(row, lanes[v]), found[c][v])
    for c in range(8):
        both = jnp.concatenate(found[c], axis=0) if c < 6 else jnp.zeros((16, 128), F32)
        at = 0
        for out in outs:
            size = out.shape[0]
            out[:, c, :] = both[at : at + size, :]
            at += size


def one_hot_matmul(acc_ref, a_ref, b_ref):
    return lax.dot_general(
        a_ref[...], b_ref[...], (((1,), (1,)), ((), ())), preferred_element_type=F32
    )


def split(value):
    high = value.astype(BF16).astype(F32)
    return high, value - high


def lists_kernel(field_ref, picks_ref, *outs):
    pick_lists(field_ref, picks_ref, outs)


def beam_kernel(
    n,
    field_ref,
    near_ref,
    other_ref,
    slots_ref,
    shape_ref,
    kind_ref,
    weight_ref,
    stiff_ref,
    own_ref,
    own_near_ref,
    send_ref,
    ends_ref,
    val_ref,
    a_ref,
    b_ref,
    acc_ref,
):
    def gather_end(at, carry):
        e, h = at // 2, at % 2
        slots = [slots_ref[3 * e + k, h] for k in range(3)]
        lanes = [s & 127 for s in slots]
        rows = [lax.shift_right_logical(s, 7) for s in slots]
        found = [[jnp.zeros((8, 128), F32) for _ in range(3)] for _ in range(6)]
        tables = []
        for rel in range(8):
            for half in range(2):
                tables.append((rel, half, lambda c, k=rel, h2=half: field_ref[2 * c + h2, k : k + 1, :]))
                tables.append((8 + rel, half, lambda c, k=rel, h2=half: other_ref[2 * c + h2, k : k + 1, :]))
        for d in range(n):
            for half in range(2):
                tables.append((16 + d, half, lambda c, k=2 * d + half: near_ref[k, c : c + 1, :]))
                tables.append((24 + d, half, lambda c, k=2 * d + half: other_ref[12 + k, c : c + 1, :]))
        for rel, half, load in tables:
            hit = [r == 2 * rel + half for r in rows]
            for c in range(6):
                row = spread(load(c))
                for k in range(3):
                    found[c][k] = jnp.where(hit[k], lane_pick(row, lanes[k]), found[c][k])
        shapes = [shape_ref[3 * e + k, h] for k in range(3)]
        for c in range(6):
            ends_ref[h, e * 6 + c] = sum(found[c][k] * shapes[k] for k in range(3))
        return carry

    lax.fori_loop(0, 4, gather_end, 0)

    def forces(h, carry):
        kind = kind_ref[h]
        weight = weight_ref[h]
        vec = [ends_ref[h, j] for j in range(12)]
        for e in range(2):
            scaled = [shape_ref[3 * e + k, h] * weight for k in range(3)]
            for i in range(6):
                total = jnp.zeros((8, 128), F32)
                for j in range(12):
                    at = (6 * e + i) * 12 + j
                    total += lane_pick(spread(stiff_ref[at : at + 1, :]), kind) * vec[j]
                for k in range(3):
                    high, low = split(scaled[k] * total)
                    val_ref[3 * e + k, 0, i, h] = high
                    val_ref[3 * e + k, 1, i, h] = low
        return carry

    lax.fori_loop(0, 2, forces, 0)

    acc_ref[...] = jnp.zeros_like(acc_ref)
    iota_hi = lax.broadcasted_iota(jnp.int32, (32, 128), 0)
    iota_lo = lax.broadcasted_iota(jnp.int32, (256, 128), 0)

    def scatter(j, carry):
        for h in range(2):
            for q in range(8):
                slot = slots_ref[j, h, q : q + 1, :]
                hit = iota_hi == lax.shift_right_logical(slot, 8)
                at = (8 * h + q) * 128
                for part in range(2):
                    for c in range(6):
                        row = val_ref[j, part, c, h, q : q + 1, :]
                        a_ref[part * 192 + c * 32 : part * 192 + (c + 1) * 32, at : at + 128] = jnp.where(
                            hit, jnp.broadcast_to(row, (32, 128)), 0.0
                        ).astype(BF16)
                b_ref[:, at : at + 128] = jnp.where(iota_lo == (slot & 255), 1.0, 0.0).astype(BF16)
        acc_ref[...] += one_hot_matmul(acc_ref, a_ref, b_ref)
        return carry

    lax.fori_loop(0, 6, scatter, 0)
    for c in range(6):
        total = acc_ref[c * 32 : (c + 1) * 32, :] + acc_ref[192 + c * 32 : 192 + (c + 1) * 32, :]
        for half in range(2):
            part = total[:, half * 128 : (half + 1) * 128]
            own_ref[2 * c + half] = part[0:8]
            send_ref[2 * c + half] = part[8:16]
            for d in range(n):
                own_near_ref[2 * d + half, c : c + 1, :] = part[16 + d : 17 + d]
                send_ref[12 + 2 * d + half, c : c + 1, :] = part[24 + d : 25 + d]
    for k in range(2 * n):
        own_near_ref[k, 6:8, :] = jnp.zeros((2, 128), F32)
        send_ref[12 + k, 6:8, :] = jnp.zeros((2, 128), F32)


def update_kernel(
    n_returns,
    last,
    own_ref,
    recv_ref,
    field_ref,
    velocity_ref,
    mass_ref,
    picks_ref,
    *refs,
):
    returns, refs = refs[:n_returns], refs[n_returns:]
    new_field_ref, new_velocity_ref = refs[0], refs[1]
    a_ref, b_ref = refs[-2], refs[-1]
    outs = refs[2:-2]
    iota_hi = lax.broadcasted_iota(jnp.int32, (8, 128), 0)
    iota_lo = lax.broadcasted_iota(jnp.int32, (256, 128), 0)
    p = 0
    for ret in returns:
        for k in range(ret.shape[0]):
            pick = picks_ref[p : p + 1, :]
            hit = iota_hi == lax.shift_right_logical(pick, 8)
            at = p * 128
            value = ret[k]
            parts = [[], []]
            for part, piece in enumerate(split(value)):
                for c in range(6):
                    parts[part].append(jnp.where(hit, spread(piece[c : c + 1, :]), 0.0))
            a_ref[:, at : at + 128] = jnp.concatenate(parts[0] + parts[1], axis=0).astype(BF16)
            b_ref[:, at : at + 128] = jnp.where(iota_lo == (pick & 255), 1.0, 0.0).astype(BF16)
            p += 1
    back = one_hot_matmul(None, a_ref, b_ref)
    back = back[:48] + back[48:]
    for c in range(6):
        for half in range(2):
            at = 2 * c + half
            force = (
                own_ref[at] + recv_ref[at] + back[c * 8 : (c + 1) * 8, half * 128 : (half + 1) * 128]
            )
            velocity = 0.98 * velocity_ref[at] - 0.2 * force / mass_ref[half]
            new_velocity_ref[at] = velocity
            new_field_ref[at] = field_ref[at] + 0.2 * velocity
    if not last:
        pick_lists(new_field_ref, picks_ref, outs)


def pairs(count, shift):
    out = []
    for i in range(shift, count - 1, 2):
        out += [(i, i + 1), (i + 1, i)]
    return out


def f32_out(*shape):
    return jax.ShapeDtypeStruct(shape, F32)


def params():
    return pltpu.CompilerParams(vmem_limit_bytes=48 * 1024 * 1024)


def shards(
    displace,
    velocity,
    nodal_mass,
    send_list,
    beam_slots,
    shape_values,
    beam_kind,
    cluster_weight,
    stiffness,
):
    list_len = send_list.shape[2]
    cols = lax.axis_size("cols")
    U = 2 if cols <= 2 else 3
    n = 3 * U - 1
    kinds = stiffness.shape[0]
    r_odd = lax.axis_index("rows") % 2
    c_odd = lax.axis_index("cols") % 2
    s = lax.axis_index("sub")
    row_perm = [pairs(lax.axis_size("rows"), 0), pairs(lax.axis_size("rows"), 1)]
    col_perm = [pairs(cols, 0), pairs(cols, 1)][: U - 1]
    sub_perm = [(0, 1), (1, 0)]

    def blocked(x):
        return x.reshape(6, 8, 2, 128).transpose(0, 2, 1, 3).reshape(12, 8, 128)

    def flat(x):
        return x.reshape(6, 2, 8, 128).transpose(0, 2, 1, 3).reshape(6, 2048)

    row_order = jnp.where(r_odd == 0, send_list[::-1], send_list)
    ordered = jnp.where(c_odd == 0, row_order[:, ::-1], row_order)
    rows_of = [ordered[0], ordered[2], ordered[1]]
    col_at = [1, 0, 2][:U]
    picks = [rows_of[t][u] for t in range(2) for u in col_at] + [rows_of[2][u] for u in col_at[1:]]
    picks = jnp.stack(picks).reshape(2 * n, 128)
    if 2 * n < 16:
        picks = jnp.concatenate([picks, jnp.zeros((16 - 2 * n, 128), jnp.int32)], axis=0)

    slots = beam_slots.reshape(6, 2, 8, 128)
    hi = slots >> 8
    remote = hi - 16
    sender = (remote >= 9).astype(jnp.int32)
    direction = remote - 9 * sender
    a = (direction >= 3).astype(jnp.int32) + (direction >= 6).astype(jnp.int32)
    b = direction - 3 * a
    a = jnp.where(r_odd == 0, a, 2 - a)
    b = jnp.where(c_odd == 0, b, 2 - b)
    t = jnp.where(a == 1, 2, a >> 1)
    u = jnp.where(b == 1, 0, (b >> 1) + 1)
    order = jnp.where(t == 2, 2 * U + u - 1, t * U + u)
    rel_near = 16 + 8 * (sender ^ s) + order
    rel_near = jnp.where(u < U, rel_near, 64)
    rel = jnp.where(hi < 16, hi ^ (8 * s), rel_near)
    slots = rel * 256 + (slots & 255)

    shapes = shape_values.reshape(6, 2, 8, 128)
    kind = beam_kind.reshape(2, 8, 128)
    weight = cluster_weight.reshape(2, 8, 128)
    stiff = jnp.pad(stiffness.reshape(kinds, 144).T, ((0, 0), (0, 128 - kinds)))
    mass = nodal_mass.reshape(8, 2, 128).transpose(1, 0, 2)

    field = blocked(displace)
    speed = blocked(velocity)
    list_outs = [f32_out(2 * U, 8, 128), f32_out(2 * U, 8, 128), f32_out(2 * U - 2, 8, 128)]
    outgoing = pl.pallas_call(
        lists_kernel,
        out_shape=list_outs,
        in_specs=[VMEM] * 2,
        out_specs=[VMEM] * 3,
        compiler_params=params(),
    )(field, picks)
    for step in range(STEPS):
        to_rows, own_row = outgoing[:2], outgoing[2]
        arrived = [lax.ppermute(x, "rows", perm) for x, perm in zip(to_rows, row_perm)]
        near = [[x[0:2]] for x in arrived] + [[]]
        for u in range(1, U):
            at = 2 * u
            message = jnp.concatenate(
                [arrived[0][at : at + 2], arrived[1][at : at + 2], own_row[at - 2 : at]], axis=0
            )
            got = lax.ppermute(message, "cols", col_perm[u - 1])
            for t in range(3):
                near[t].append(got[2 * t : 2 * t + 2])
        near = jnp.concatenate(near[0] + near[1] + near[2], axis=0)
        other = lax.ppermute(jnp.concatenate([field, near], axis=0), "sub", sub_perm)
        own, own_near, send = pl.pallas_call(
            functools.partial(beam_kernel, n),
            out_shape=[f32_out(12, 8, 128), f32_out(2 * n, 8, 128), f32_out(12 + 2 * n, 8, 128)],
            in_specs=[VMEM] * 8,
            out_specs=[VMEM] * 3,
            scratch_shapes=[
                pltpu.VMEM((2, 12, 8, 128), F32),
                pltpu.VMEM((6, 2, 6, 2, 8, 128), F32),
                pltpu.VMEM((384, 2048), BF16),
                pltpu.VMEM((256, 2048), BF16),
                pltpu.VMEM((384, 256), F32),
            ],
            compiler_params=params(),
        )(field, near, other, slots, shapes, kind, weight, stiff)
        recv = lax.ppermute(send, "sub", sub_perm)
        total = own_near + recv[12:]

        def listed(t, u):
            at = 2 * (t * U + u) if t < 2 else 2 * (2 * U + u - 1)
            return total[at : at + 2]

        back_rows = [[listed(0, 0)], [listed(1, 0)]]
        back_own = []
        for u in range(1, U):
            message = jnp.concatenate([listed(t, u) for t in range(3)], axis=0)
            got = lax.ppermute(message, "cols", col_perm[u - 1])
            back_rows[0].append(got[0:2])
            back_rows[1].append(got[2:4])
            back_own.append(got[4:6])
        returns = [
            lax.ppermute(jnp.concatenate(x, axis=0), "rows", perm)
            for x, perm in zip(back_rows, row_perm)
        ] + [jnp.concatenate(back_own, axis=0)]
        last = step == STEPS - 1
        outs = pl.pallas_call(
            functools.partial(update_kernel, 3, last),
            out_shape=[f32_out(12, 8, 128)] * 2 + ([] if last else list_outs),
            in_specs=[VMEM] * 9,
            out_specs=[VMEM] * (2 if last else 5),
            scratch_shapes=[pltpu.VMEM((96, 256 * n), BF16), pltpu.VMEM((256, 256 * n), BF16)],
            compiler_params=params(),
        )(own, recv, field, speed, mass, picks, *returns)
        field, speed = outs[:2]
        outgoing = outs[2:]
    return flat(field), flat(speed)


def solution(mesh):
    whole = ("groups", "rows", "cols", "sub")
    in_specs = (
        P(None, whole),
        P(None, whole),
        P(whole),
        P("rows", "cols", ("groups", "sub")),
        P(None, whole),
        P(None, whole),
        P(whole),
        P(whole),
        P(),
    )
    out_specs = (P(None, whole), P(None, whole))
    return jax.shard_map(shards, mesh=mesh, in_specs=in_specs, out_specs=out_specs, check_vma=False)
```

```python
import functools

import jax
import jax.numpy as jnp
from jax import lax
from jax.experimental import pallas as pl
from jax.experimental.pallas import tpu as pltpu
from jax.sharding import PartitionSpec as P

STEPS = 2
F32 = jnp.float32
BF16 = jnp.bfloat16
VMEM = pl.BlockSpec(memory_space=pltpu.VMEM)


def lane_pick(row, lanes):
    return jnp.take_along_axis(row, lanes, axis=1, mode="promise_in_bounds")


def spread(row):
    return jnp.broadcast_to(row, (8, 128))


def split(value):
    high = value.astype(BF16).astype(F32)
    return high, value - high


def padded(tile):
    return jnp.concatenate([tile, jnp.zeros((8 - tile.shape[0], 128), F32)], axis=0)


def pick_lists(field_ref, picks_ref, outs):
    picks = [picks_ref[0:8, :], picks_ref[8:16, :]]
    lanes = [p & 127 for p in picks]
    rows = [lax.shift_right_logical(p, 7) for p in picks]
    found = [[jnp.zeros((8, 128), F32) for _ in range(2)] for _ in range(6)]
    for tile in range(16):
        hit = [r == tile for r in rows]
        for c in range(6):
            row = spread(field_ref[tile, c : c + 1, :])
            for v in range(2):
                found[c][v] = jnp.where(hit[v], lane_pick(row, lanes[v]), found[c][v])
    for c in range(8):
        both = jnp.concatenate(found[c], axis=0) if c < 6 else jnp.zeros((16, 128), F32)
        at = 0
        for out in outs:
            size = out.shape[0]
            out[:, c, :] = both[at : at + size, :]
            at += size


def lists_kernel(displace_ref, picks_ref, field_ref, *outs):
    for tile in range(16):
        field_ref[tile] = padded(displace_ref[:, tile * 128 : (tile + 1) * 128])
    pick_lists(field_ref, picks_ref, outs)


def one_hot(lanes):
    iota = lax.broadcasted_iota(jnp.int32, (256, 128), 0)
    return jnp.where(iota == lanes, 1.0, 0.0).astype(BF16)


def times_one_hot(values, hot):
    return lax.dot_general(values, hot, (((1,), (1,)), ((), ())), preferred_element_type=F32)


def beam_kernel(
    n,
    kinds,
    field_ref,
    near_ref,
    other_ref,
    slots_ref,
    shape_ref,
    kind_ref,
    weight_ref,
    stiff_ref,
    own_ref,
    own_near_ref,
    send_ref,
    table_ref,
    hot_ref,
    x_ref,
    vec_ref,
    cat_ref,
    force_ref,
    a_ref,
    acc_ref,
):
    rows = 16 + 2 * n
    low_at = rows * 8

    def tile_of(row, half):
        if row < 8:
            return field_ref[2 * row + half]
        if row < 16:
            return other_ref[2 * (row - 8) + half]
        if row < 16 + n:
            return near_ref[2 * (row - 16) + half]
        return other_ref[2 * (row - 8 - n) + half]

    for row in range(0, rows, 2):
        for half in range(2):
            high, low = split(jnp.concatenate([tile_of(row, half), tile_of(row + 1, half)], axis=0))
            table_ref[row * 8 : row * 8 + 16, half * 128 : (half + 1) * 128] = high.astype(BF16)
            table_ref[low_at + row * 8 : low_at + row * 8 + 16, half * 128 : (half + 1) * 128] = low.astype(BF16)

    def gather(g, carry):
        col = pl.multiple_of(g * 256, 256)
        start = pl.multiple_of(g * 1536, 1536)
        slots = slots_ref[:, pl.ds(col, 256)]
        shape = shape_ref[:, pl.ds(col, 256)]
        for bb in range(2):
            for j in range(6):
                slot = slots[j : j + 1, bb * 128 : (bb + 1) * 128]
                hot_ref[:, pl.ds(start + (bb * 6 + j) * 128, 128)] = one_hot(slot & 255)
        x_ref[...] = jnp.dot(table_ref[...], hot_ref[:, pl.ds(start, 1536)], preferred_element_type=F32)
        for bb in range(2):
            for e in range(2):
                end = jnp.zeros((8, 128), F32)
                for k in range(3):
                    j = 3 * e + k
                    hi = spread(lax.shift_right_logical(slots[j : j + 1, bb * 128 : (bb + 1) * 128], 8))
                    at = (bb * 6 + j) * 128
                    found = jnp.zeros((8, 128), F32)
                    for row in range(rows):
                        both = (
                            x_ref[row * 8 : row * 8 + 8, at : at + 128]
                            + x_ref[low_at + row * 8 : low_at + row * 8 + 8, at : at + 128]
                        )
                        found = jnp.where(hi == row, both, found)
                    end += found * spread(shape[j : j + 1, bb * 128 : (bb + 1) * 128])
                vec_ref[e * 8 : (e + 1) * 8, pl.ds(col + bb * 128, 128)] = end
        return carry

    lax.fori_loop(0, 8, gather, 0)

    v1, rest = split(vec_ref[...])
    v2, v3 = split(rest)
    for at, piece in enumerate((v1, v2, v1, v2, v3, v1)):
        cat_ref[at * 16 : (at + 1) * 16, :] = piece.astype(BF16)
    s1, rest = split(stiff_ref[...])
    s2, s3 = split(rest)
    block = lax.broadcasted_iota(jnp.int32, s1.shape, 1) // 16
    stiff = jnp.where((block == 2) | (block == 3), s2, jnp.where(block == 5, s3, s1)).astype(BF16)
    force_ref[...] = jnp.dot(stiff, cat_ref[...], preferred_element_type=F32)

    acc_ref[...] = jnp.zeros_like(acc_ref)

    def scatter(g, carry):
        col = pl.multiple_of(g * 256, 256)
        start = pl.multiple_of(g * 1536, 1536)
        slots = slots_ref[:, pl.ds(col, 256)]
        shape = shape_ref[:, pl.ds(col, 256)]
        for bb in range(2):
            kind = spread(kind_ref[pl.ds(2 * g + bb, 1), :])
            weight = weight_ref[pl.ds(2 * g + bb, 1), :]
            for e in range(2):
                force = jnp.zeros((8, 128), F32)
                for t in range(kinds):
                    force = jnp.where(
                        kind == t,
                        force_ref[t * 16 + e * 8 : t * 16 + e * 8 + 8, pl.ds(col + bb * 128, 128)],
                        force,
                    )
                for k in range(3):
                    j = 3 * e + k
                    at = (bb * 6 + j) * 128
                    hi = spread(lax.shift_right_logical(slots[j : j + 1, bb * 128 : (bb + 1) * 128], 8))
                    high, low = split(force * spread(shape[j : j + 1, bb * 128 : (bb + 1) * 128] * weight))
                    for row in range(0, rows, 2):
                        hit = [hi == row, hi == row + 1]
                        for base, piece in ((0, high), (low_at, low)):
                            a_ref[base + row * 8 : base + row * 8 + 16, at : at + 128] = jnp.concatenate(
                                [jnp.where(hit[0], piece, 0.0), jnp.where(hit[1], piece, 0.0)], axis=0
                            ).astype(BF16)
        acc_ref[...] += times_one_hot(a_ref[...], hot_ref[:, pl.ds(start, 1536)])
        return carry

    lax.fori_loop(0, 8, scatter, 0)
    for row in range(rows):
        total = acc_ref[row * 8 : row * 8 + 8, :] + acc_ref[low_at + row * 8 : low_at + row * 8 + 8, :]
        for half in range(2):
            part = total[:, half * 128 : (half + 1) * 128]
            if row < 8:
                own_ref[2 * row + half] = part
            elif row < 16:
                send_ref[2 * (row - 8) + half] = part
            elif row < 16 + n:
                own_near_ref[2 * (row - 16) + half] = part
            else:
                send_ref[2 * (row - 8 - n) + half] = part


def update_kernel(n_returns, last, own_ref, recv_ref, field_ref, velocity_ref, mass_ref, picks_ref, *refs):
    returns, refs = refs[:n_returns], refs[n_returns:]
    new_field_ref, new_velocity_ref = refs[0], refs[1]
    a_ref, b_ref = refs[-2], refs[-1]
    outs = refs[2:-2]
    p = 0
    for ret in returns:
        for tile in range(ret.shape[0]):
            pick = picks_ref[p : p + 1, :]
            hi = spread(lax.shift_right_logical(pick, 8))
            at = p * 128
            for base, piece in zip((0, 64), split(ret[tile])):
                a_ref[base : base + 64, at : at + 128] = jnp.concatenate(
                    [jnp.where(hi == row, piece, 0.0) for row in range(8)], axis=0
                ).astype(BF16)
            b_ref[:, at : at + 128] = one_hot(pick & 255)
            p += 1
    back = times_one_hot(a_ref[...], b_ref[...])
    back = back[:64] + back[64:]
    for tile in range(16):
        row, half = tile // 2, tile % 2
        cols = slice(tile * 128, (tile + 1) * 128)
        force = own_ref[tile] + recv_ref[tile] + back[row * 8 : row * 8 + 8, half * 128 : (half + 1) * 128]
        velocity = 0.98 * velocity_ref[:, cols] - 0.2 * force[0:6] / mass_ref[:, cols]
        new_velocity_ref[:, cols] = velocity
        field = field_ref[tile][0:6] + 0.2 * velocity
        if last:
            new_field_ref[:, cols] = field
        else:
            new_field_ref[tile] = padded(field)
    if not last:
        pick_lists(new_field_ref, picks_ref, outs)


def pairs(count, shift):
    out = []
    for i in range(shift, count - 1, 2):
        out += [(i, i + 1), (i + 1, i)]
    return out


def f32_out(*shape):
    return jax.ShapeDtypeStruct(shape, F32)


def params():
    return pltpu.CompilerParams(vmem_limit_bytes=48 * 1024 * 1024)


def shards(
    displace,
    velocity,
    nodal_mass,
    send_list,
    beam_slots,
    shape_values,
    beam_kind,
    cluster_weight,
    stiffness,
):
    list_len = send_list.shape[2]
    cols = lax.axis_size("cols")
    U = 2 if cols <= 2 else 3
    n = 3 * U - 1
    rows = 16 + 2 * n
    kinds = stiffness.shape[0]
    r_odd = lax.axis_index("rows") % 2
    c_odd = lax.axis_index("cols") % 2
    s = lax.axis_index("sub")
    row_perm = [pairs(lax.axis_size("rows"), 0), pairs(lax.axis_size("rows"), 1)]
    col_perm = [pairs(cols, 0), pairs(cols, 1)][: U - 1]
    sub_perm = [(0, 1), (1, 0)]

    row_order = jnp.where(r_odd == 0, send_list[::-1], send_list)
    ordered = jnp.where(c_odd == 0, row_order[:, ::-1], row_order)
    rows_of = [ordered[0], ordered[2], ordered[1]]
    col_at = [1, 0, 2][:U]
    picks = [rows_of[t][u] for t in range(2) for u in col_at] + [rows_of[2][u] for u in col_at[1:]]
    picks = jnp.stack(picks).reshape(2 * n, 128)
    if 2 * n < 16:
        picks = jnp.concatenate([picks, jnp.zeros((16 - 2 * n, 128), jnp.int32)], axis=0)

    slots = beam_slots
    hi = slots >> 8
    remote = hi - 16
    sender = (remote >= 9).astype(jnp.int32)
    direction = remote - 9 * sender
    a = (direction >= 3).astype(jnp.int32) + (direction >= 6).astype(jnp.int32)
    b = direction - 3 * a
    a = jnp.where(r_odd == 0, a, 2 - a)
    b = jnp.where(c_odd == 0, b, 2 - b)
    t = jnp.where(a == 1, 2, a >> 1)
    u = jnp.where(b == 1, 0, (b >> 1) + 1)
    order = jnp.where(t == 2, 2 * U + u - 1, t * U + u)
    rel_near = 16 + n * (sender ^ s) + order
    rel_near = jnp.where(u < U, rel_near, 64)
    rel = jnp.where(hi < 16, hi ^ (8 * s), rel_near)
    slots = rel * 256 + (slots & 255)

    kind = beam_kind.reshape(16, 128)
    weight = cluster_weight.reshape(16, 128)
    stiff = jnp.pad(stiffness.reshape(kinds, 2, 6, 2, 6), ((0, 0), (0, 0), (0, 2), (0, 0), (0, 2)))
    stiff = jnp.tile(stiff.reshape(kinds * 16, 16), (1, 6))
    mass = nodal_mass.reshape(1, -1)

    speed = velocity
    list_outs = [f32_out(2 * U, 8, 128), f32_out(2 * U, 8, 128), f32_out(2 * U - 2, 8, 128)]
    field, *outgoing = pl.pallas_call(
        lists_kernel,
        out_shape=[f32_out(16, 8, 128)] + list_outs,
        in_specs=[VMEM] * 2,
        out_specs=[VMEM] * 4,
        compiler_params=params(),
    )(displace, picks)
    for step in range(STEPS):
        to_rows, own_row = outgoing[:2], outgoing[2]
        arrived = [lax.ppermute(x, "rows", perm) for x, perm in zip(to_rows, row_perm)]
        near = [[x[0:2]] for x in arrived] + [[]]
        for u in range(1, U):
            at = 2 * u
            message = jnp.concatenate(
                [arrived[0][at : at + 2], arrived[1][at : at + 2], own_row[at - 2 : at]], axis=0
            )
            got = lax.ppermute(message, "cols", col_perm[u - 1])
            for t in range(3):
                near[t].append(got[2 * t : 2 * t + 2])
        near = jnp.concatenate(near[0] + near[1] + near[2], axis=0)
        other = lax.ppermute(jnp.concatenate([field, near], axis=0), "sub", sub_perm)
        own, own_near, send = pl.pallas_call(
            functools.partial(beam_kernel, n, kinds),
            out_shape=[f32_out(16, 8, 128), f32_out(2 * n, 8, 128), f32_out(16 + 2 * n, 8, 128)],
            in_specs=[VMEM] * 8,
            out_specs=[VMEM] * 3,
            scratch_shapes=[
                pltpu.VMEM((16 * rows, 256), BF16),
                pltpu.VMEM((256, 12288), BF16),
                pltpu.VMEM((16 * rows, 1536), F32),
                pltpu.VMEM((16, 2048), F32),
                pltpu.VMEM((96, 2048), BF16),
                pltpu.VMEM((16 * kinds, 2048), F32),
                pltpu.VMEM((16 * rows, 1536), BF16),
                pltpu.VMEM((16 * rows, 256), F32),
            ],
            compiler_params=params(),
        )(field, near, other, slots, shape_values, kind, weight, stiff)
        recv = lax.ppermute(send, "sub", sub_perm)
        total = own_near + recv[16:]

        def listed(t, u):
            at = 2 * (t * U + u) if t < 2 else 2 * (2 * U + u - 1)
            return total[at : at + 2]

        back_rows = [[listed(0, 0)], [listed(1, 0)]]
        back_own = []
        for u in range(1, U):
            message = jnp.concatenate([listed(t, u) for t in range(3)], axis=0)
            got = lax.ppermute(message, "cols", col_perm[u - 1])
            back_rows[0].append(got[0:2])
            back_rows[1].append(got[2:4])
            back_own.append(got[4:6])
        returns = [
            lax.ppermute(jnp.concatenate(x, axis=0), "rows", perm)
            for x, perm in zip(back_rows, row_perm)
        ] + [jnp.concatenate(back_own, axis=0)]
        last = step == STEPS - 1
        outs = pl.pallas_call(
            functools.partial(update_kernel, 3, last),
            out_shape=[f32_out(6, 2048)] * 2 if last else [f32_out(16, 8, 128), f32_out(6, 2048)] + list_outs,
            in_specs=[VMEM] * 9,
            out_specs=[VMEM] * (2 if last else 5),
            scratch_shapes=[pltpu.VMEM((128, 256 * n), BF16), pltpu.VMEM((256, 256 * n), BF16)],
            compiler_params=params(),
        )(own, recv, field, speed, mass, picks, *returns)
        field, speed = outs[:2]
        outgoing = outs[2:]
    return field, speed


def solution(mesh):
    whole = ("groups", "rows", "cols", "sub")
    in_specs = (
        P(None, whole),
        P(None, whole),
        P(whole),
        P("rows", "cols", ("groups", "sub")),
        P(None, whole),
        P(None, whole),
        P(whole),
        P(whole),
        P(),
    )
    out_specs = (P(None, whole), P(None, whole))
    return jax.shard_map(shards, mesh=mesh, in_specs=in_specs, out_specs=out_specs, check_vma=False)
```

```python
import functools

import jax
import jax.numpy as jnp
from jax import lax
from jax.experimental import pallas as pl
from jax.experimental.pallas import tpu as pltpu
from jax.sharding import PartitionSpec as P

STEPS = 2
F32 = jnp.float32
BF16 = jnp.bfloat16
VMEM = pl.BlockSpec(memory_space=pltpu.VMEM)


def lane_pick(row, lanes):
    return jnp.take_along_axis(row, lanes, axis=1, mode="promise_in_bounds")


def spread(row):
    return jnp.broadcast_to(row, (8, 128))


def split(value):
    high = value.astype(BF16).astype(F32)
    return high, value - high


def padded(tile):
    return jnp.concatenate([tile, jnp.zeros((8 - tile.shape[0], 128), F32)], axis=0)


def pick_lists(field_ref, picks_ref, outs):
    picks = [picks_ref[0:8, :], picks_ref[8:16, :]]
    lanes = [p & 127 for p in picks]
    rows = [lax.shift_right_logical(p, 7) for p in picks]
    found = [[jnp.zeros((8, 128), F32) for _ in range(2)] for _ in range(6)]
    for tile in range(16):
        hit = [r == tile for r in rows]
        for c in range(6):
            row = spread(field_ref[tile, c : c + 1, :])
            for v in range(2):
                found[c][v] = jnp.where(hit[v], lane_pick(row, lanes[v]), found[c][v])
    for c in range(8):
        both = jnp.concatenate(found[c], axis=0) if c < 6 else jnp.zeros((16, 128), F32)
        at = 0
        for out in outs:
            size = out.shape[0]
            out[:, c, :] = both[at : at + size, :]
            at += size


def lists_kernel(U, odd_ref, displace_ref, send_ref, field_ref, picks_ref, *outs):
    r_odd, c_odd = odd_ref[0], odd_ref[1]
    swap = [jnp.where(r_odd == 0, send_ref[2 * t], send_ref[2 - 2 * t]) for t in (1, 0)] + [send_ref[1]]
    at = 0
    for t in range(3):
        lists = [swap[t][1:2]]
        lists += [jnp.where(c_odd == 0, swap[t][2 * u : 2 * u + 1], swap[t][2 - 2 * u : 3 - 2 * u]) for u in (1, 0)]
        for u in range(U):
            if t < 2 or u > 0:
                for half in range(2):
                    picks_ref[at : at + 1, :] = lists[u][:, half * 128 : (half + 1) * 128]
                    at += 1
    if at < 16:
        picks_ref[at:16, :] = jnp.zeros((16 - at, 128), jnp.int32)
    for tile in range(16):
        field_ref[tile] = padded(displace_ref[:, tile * 128 : (tile + 1) * 128])
    pick_lists(field_ref, picks_ref, outs)


def one_hot(lanes):
    lanes = jnp.broadcast_to(lanes.astype(F32), (16, 128)).astype(BF16)
    iota = lax.broadcasted_iota(jnp.int32, (16, 128), 0).astype(F32)
    one, zero = jnp.ones((16, 128), BF16), jnp.zeros((16, 128), BF16)
    return jnp.concatenate(
        [jnp.where((iota + 16.0 * at).astype(BF16) == lanes, one, zero) for at in range(16)], axis=0
    )


def times_one_hot(values, hot):
    return lax.dot_general(values, hot, (((1,), (1,)), ((), ())), preferred_element_type=F32)


def build_hot(e, quad, slots_ref, hot_ref):
    for bb in range(4):
        b = quad * 4 + bb
        for k in range(3):
            slot = slots_ref[3 * e + k : 3 * e + k + 1, b * 128 : (b + 1) * 128]
            at = (e * 48 + b * 3 + k) * 128
            hot_ref[:, at : at + 128] = one_hot(slot & 255)


def fill_table(tiles, table_ref):
    low_at = len(tiles) * 8
    for row in range(0, len(tiles), 2):
        for half in range(2):
            both = jnp.concatenate([tiles[row](half), tiles[row + 1](half)], axis=0)
            for base, piece in zip((0, low_at), split(both)):
                table_ref[base + row * 8 : base + row * 8 + 16, half * 128 : (half + 1) * 128] = piece.astype(BF16)


def gather_step(e, quad, first, rows, table_ref, hot_ref, x_refs, slots_ref, shape_ref, vec_ref, base_ref=None):
    low_at = rows * 8
    start = (4 * e + quad) * 1536
    x_ref = x_refs.at[quad % 2]
    x_ref[...] = jnp.dot(table_ref[...], hot_ref[:, start : start + 1536], preferred_element_type=F32)
    for bb in range(4):
        b = quad * 4 + bb
        cols = slice(b * 128, (b + 1) * 128)
        end = jnp.zeros((8, 128), F32) if base_ref is None else base_ref[:, cols]
        for k in range(3):
            j = 3 * e + k
            hi = spread(lax.shift_right_logical(slots_ref[j : j + 1, cols], 8))
            at = (bb * 3 + k) * 128
            found = jnp.zeros((8, 128), F32)
            for row in range(rows):
                high = x_ref[row * 8 : row * 8 + 8, at : at + 128]
                low = x_ref[low_at + row * 8 : low_at + row * 8 + 8, at : at + 128]
                found = jnp.where(hi == first + row, high + low, found)
            end += found * spread(shape_ref[j : j + 1, cols])
        vec_ref[:, cols] = end


def scatter_step(e, quad, first, rows, force_ref, a_refs, acc_ref, hot_ref, slots_ref, shape_ref, weight_ref):
    low_at = rows * 8
    start = (4 * e + quad) * 1536
    a_ref = a_refs.at[quad % 2]
    for bb in range(4):
        b = quad * 4 + bb
        cols = slice(b * 128, (b + 1) * 128)
        force = force_ref[e * 8 : e * 8 + 8, cols]
        weight = weight_ref[b : b + 1, :]
        for k in range(3):
            j = 3 * e + k
            at = (bb * 3 + k) * 128
            hi = spread(lax.shift_right_logical(slots_ref[j : j + 1, cols], 8))
            pieces = split(force * spread(shape_ref[j : j + 1, cols] * weight))
            for row in range(0, rows, 2):
                hit = [hi == first + row, hi == first + row + 1]
                for base, piece in zip((0, low_at), pieces):
                    a_ref[base + row * 8 : base + row * 8 + 16, at : at + 128] = jnp.concatenate(
                        [jnp.where(hit[0], piece, 0.0), jnp.where(hit[1], piece, 0.0)], axis=0
                    ).astype(BF16)
    acc_ref[...] += times_one_hot(a_ref[...], hot_ref[:, start : start + 1536])


def local_gather_kernel(e, build, *refs):
    if build:
        field_ref, other_ref, slots_ref, shape_ref, vec_ref, table_ref, x_refs, hot_ref = refs
    else:
        field_ref, other_ref, slots_ref, shape_ref, hot_ref, vec_ref, table_ref, x_refs = refs
    tiles = [lambda half, k=k: field_ref[2 * k + half] for k in range(8)]
    tiles += [lambda half, k=k: other_ref[2 * k + half] for k in range(8)]
    fill_table(tiles, table_ref)
    for quad in range(4):
        if build:
            build_hot(e, quad, slots_ref, hot_ref)
        gather_step(e, quad, 0, 16, table_ref, hot_ref, x_refs, slots_ref, shape_ref, vec_ref)


def near_kernel(n, kinds, build, *refs):
    vec0_ref, vec1_ref, near_ref, other_ref, slots_ref, shape_ref, kind_ref, weight_ref, stiff_ref = refs[:9]
    if build:
        own_near_ref, send_ref, force_ref, hot_ref = refs[9:13]
    else:
        hot_ref, own_near_ref, send_ref, force_ref = refs[9:13]
    table_ref, x_refs, vec_ref, cat_ref, kinds_ref, a_refs, acc_ref = refs[13:]
    tiles = [lambda half, k=k: near_ref[2 * k + half] for k in range(n)]
    tiles += [lambda half, k=k: other_ref[2 * k + half] for k in range(n)]
    fill_table(tiles, table_ref)
    for e, base_ref in enumerate((vec0_ref, vec1_ref)):
        for quad in range(4):
            if build:
                build_hot(e, quad, slots_ref, hot_ref)
            gather_step(
                e, quad, 16, 2 * n, table_ref, hot_ref, x_refs, slots_ref, shape_ref, vec_ref.at[e], base_ref
            )

    v1, rest = split(jnp.concatenate([vec_ref[0], vec_ref[1]], axis=0))
    v2, v3 = split(rest)
    for at, piece in enumerate((v1, v2, v1, v2, v3, v1)):
        cat_ref[at * 16 : (at + 1) * 16, :] = piece.astype(BF16)
    s1, rest = split(stiff_ref[...])
    s2, s3 = split(rest)
    block = lax.broadcasted_iota(jnp.int32, s1.shape, 1) // 16
    stiff = jnp.where((block == 2) | (block == 3), s2, jnp.where(block == 5, s3, s1)).astype(BF16)
    kinds_ref[...] = jnp.dot(stiff, cat_ref[...], preferred_element_type=F32)
    for b in range(16):
        cols = slice(b * 128, (b + 1) * 128)
        kind = spread(kind_ref[b : b + 1, :])
        for e in range(2):
            force = jnp.zeros((8, 128), F32)
            for t in range(kinds):
                force = jnp.where(kind == t, kinds_ref[t * 16 + e * 8 : t * 16 + e * 8 + 8, cols], force)
            force_ref[e * 8 : (e + 1) * 8, cols] = force

    acc_ref[...] = jnp.zeros_like(acc_ref)
    for e in range(2):
        for quad in range(4):
            scatter_step(e, quad, 16, 2 * n, force_ref, a_refs, acc_ref, hot_ref, slots_ref, shape_ref, weight_ref)
    for row in range(2 * n):
        total = acc_ref[row * 8 : row * 8 + 8, :] + acc_ref[(2 * n + row) * 8 : (2 * n + row) * 8 + 8, :]
        for half in range(2):
            out, at = (own_near_ref, row) if row < n else (send_ref, row - n)
            out[2 * at + half] = total[:, half * 128 : (half + 1) * 128]


def local_scatter_kernel(force_ref, hot_ref, slots_ref, shape_ref, weight_ref, own_ref, send_ref, a_refs, acc_ref):
    acc_ref[...] = jnp.zeros_like(acc_ref)
    for e in range(2):
        for quad in range(4):
            scatter_step(e, quad, 0, 16, force_ref, a_refs, acc_ref, hot_ref, slots_ref, shape_ref, weight_ref)
    for row in range(16):
        total = acc_ref[row * 8 : row * 8 + 8, :] + acc_ref[128 + row * 8 : 128 + row * 8 + 8, :]
        for half in range(2):
            out, at = (own_ref, row) if row < 8 else (send_ref, row - 8)
            out[2 * at + half] = total[:, half * 128 : (half + 1) * 128]


def update_kernel(n_returns, last, own_ref, recv_ref, field_ref, velocity_ref, mass_ref, picks_ref, *refs):
    returns, refs = refs[:n_returns], refs[n_returns:]
    new_field_ref, new_velocity_ref = refs[0], refs[1]
    a_ref, b_ref = refs[-2], refs[-1]
    outs = refs[2:-2]
    p = 0
    for ret in returns:
        for tile in range(ret.shape[0]):
            pick = picks_ref[p : p + 1, :]
            hi = spread(lax.shift_right_logical(pick, 8))
            at = p * 128
            for base, piece in zip((0, 64), split(ret[tile])):
                a_ref[base : base + 64, at : at + 128] = jnp.concatenate(
                    [jnp.where(hi == row, piece, 0.0) for row in range(8)], axis=0
                ).astype(BF16)
            b_ref[:, at : at + 128] = one_hot(pick & 255)
            p += 1
    back = times_one_hot(a_ref[...], b_ref[...])
    back = back[:64] + back[64:]
    for tile in range(16):
        row, half = tile // 2, tile % 2
        cols = slice(tile * 128, (tile + 1) * 128)
        force = own_ref[tile] + recv_ref[tile] + back[row * 8 : row * 8 + 8, half * 128 : (half + 1) * 128]
        velocity = 0.98 * velocity_ref[:, cols] - 0.2 * force[0:6] / mass_ref[:, cols]
        new_velocity_ref[:, cols] = velocity
        field = field_ref[tile][0:6] + 0.2 * velocity
        if last:
            new_field_ref[:, cols] = field
        else:
            new_field_ref[tile] = padded(field)
    if not last:
        pick_lists(new_field_ref, picks_ref, outs)


def pairs(count, shift):
    out = []
    for i in range(shift, count - 1, 2):
        out += [(i, i + 1), (i + 1, i)]
    return out


def f32_out(*shape):
    return jax.ShapeDtypeStruct(shape, F32)


def params():
    return pltpu.CompilerParams(vmem_limit_bytes=24 * 1024 * 1024)


def cost(us):
    return pl.CostEstimate(flops=us * 10**9, bytes_accessed=us * 10**6, transcendentals=0)


def shards(
    displace,
    velocity,
    nodal_mass,
    send_list,
    beam_slots,
    shape_values,
    beam_kind,
    cluster_weight,
    stiffness,
):
    list_len = send_list.shape[2]
    cols = lax.axis_size("cols")
    U = 2 if cols <= 2 else 3
    n = 3 * U - 1
    kinds = stiffness.shape[0]
    r_odd = lax.axis_index("rows") % 2
    c_odd = lax.axis_index("cols") % 2
    s = lax.axis_index("sub")
    row_perm = [pairs(lax.axis_size("rows"), 0), pairs(lax.axis_size("rows"), 1)]
    col_perm = [pairs(cols, 0), pairs(cols, 1)][: U - 1]
    sub_perm = [(0, 1), (1, 0)]

    slots = beam_slots
    hi = slots >> 8
    remote = hi - 16
    sender = (remote >= 9).astype(jnp.int32)
    direction = remote - 9 * sender
    a = (direction >= 3).astype(jnp.int32) + (direction >= 6).astype(jnp.int32)
    b = direction - 3 * a
    a = jnp.where(r_odd == 0, a, 2 - a)
    b = jnp.where(c_odd == 0, b, 2 - b)
    t = jnp.where(a == 1, 2, a >> 1)
    u = jnp.where(b == 1, 0, (b >> 1) + 1)
    order = jnp.where(t == 2, 2 * U + u - 1, t * U + u)
    rel_near = 16 + n * (sender ^ s) + order
    rel_near = jnp.where(u < U, rel_near, 64)
    rel = jnp.where(hi < 16, hi ^ (8 * s), rel_near)
    slots = rel * 256 + (slots & 255)

    kind = beam_kind.reshape(16, 128)
    weight = cluster_weight.reshape(16, 128)
    stiff = jnp.pad(stiffness.reshape(kinds, 2, 6, 2, 6), ((0, 0), (0, 0), (0, 2), (0, 0), (0, 2)))
    stiff = jnp.tile(stiff.reshape(kinds * 16, 16), (1, 6))
    mass = nodal_mass.reshape(1, -1)

    speed = velocity
    list_outs = [f32_out(2 * U, 8, 128), f32_out(2 * U, 8, 128), f32_out(2 * U - 2, 8, 128)]
    odd = jnp.stack([r_odd, c_odd]).astype(jnp.int32)
    field, picks, *outgoing = pl.pallas_call(
        functools.partial(lists_kernel, U),
        out_shape=[f32_out(16, 8, 128), jax.ShapeDtypeStruct((16, 128), jnp.int32)] + list_outs,
        in_specs=[pl.BlockSpec(memory_space=pltpu.SMEM), VMEM, VMEM],
        out_specs=[VMEM] * 5,
        compiler_params=params(),
    )(odd, displace, send_list)
    hot = None
    tall = 32 * n
    for step in range(STEPS):
        other = lax.ppermute(field, "sub", sub_perm)

        build = hot is None

        def local_gather(e):
            return pl.pallas_call(
                functools.partial(local_gather_kernel, e, build),
                out_shape=f32_out(8, 2048),
                in_specs=[VMEM] * (4 if build else 5),
                out_specs=VMEM,
                scratch_shapes=[pltpu.VMEM((256, 256), BF16), pltpu.VMEM((2, 256, 1536), F32)]
                + ([pltpu.VMEM((256, 12288), BF16)] if build else []),
                compiler_params=params(),
                cost_estimate=cost(2),
            )(field, other, slots, shape_values, *([] if build else [hot]))

        to_rows, own_row = outgoing[:2], outgoing[2]
        arrived = [lax.ppermute(x, "rows", perm) for x, perm in zip(to_rows, row_perm)]
        vec0 = local_gather(0)
        arrived[0], arrived[1], vec0 = lax.optimization_barrier((arrived[0], arrived[1], vec0))
        near = [[x[0:2]] for x in arrived] + [[]]
        for u in range(1, U):
            at = 2 * u
            message = jnp.concatenate(
                [arrived[0][at : at + 2], arrived[1][at : at + 2], own_row[at - 2 : at]], axis=0
            )
            got = lax.ppermute(message, "cols", col_perm[u - 1])
            for t in range(3):
                near[t].append(got[2 * t : 2 * t + 2])
        near = jnp.concatenate(near[0] + near[1] + near[2], axis=0)
        vec1 = local_gather(1)
        near, vec1 = lax.optimization_barrier((near, vec1))
        near_other = lax.ppermute(near, "sub", sub_perm)
        own_near, near_send, force, *made = pl.pallas_call(
            functools.partial(near_kernel, n, kinds, build),
            out_shape=[f32_out(2 * n, 8, 128), f32_out(2 * n, 8, 128), f32_out(16, 2048)]
            + ([jax.ShapeDtypeStruct((256, 12288), BF16)] if build else []),
            in_specs=[VMEM] * (9 if build else 10),
            out_specs=[VMEM] * (4 if build else 3),
            scratch_shapes=[
                pltpu.VMEM((tall, 256), BF16),
                pltpu.VMEM((2, tall, 1536), F32),
                pltpu.VMEM((2, 8, 2048), F32),
                pltpu.VMEM((96, 2048), BF16),
                pltpu.VMEM((16 * kinds, 2048), F32),
                pltpu.VMEM((2, tall, 1536), BF16),
                pltpu.VMEM((tall, 256), F32),
            ],
            compiler_params=params(),
            cost_estimate=cost(5),
        )(vec0, vec1, near, near_other, slots, shape_values, kind, weight, stiff, *([] if build else [hot]))
        hot = made[0] if build else hot

        def local_scatter():
            return pl.pallas_call(
                local_scatter_kernel,
                out_shape=[f32_out(16, 8, 128)] * 2,
                in_specs=[VMEM] * 5,
                out_specs=[VMEM] * 2,
                scratch_shapes=[pltpu.VMEM((2, 256, 1536), BF16), pltpu.VMEM((256, 256), F32)],
                compiler_params=params(),
                cost_estimate=cost(3),
            )(force, hot, slots, shape_values, weight)

        total = own_near + lax.ppermute(near_send, "sub", sub_perm)

        def listed(t, u):
            at = 2 * (t * U + u) if t < 2 else 2 * (2 * U + u - 1)
            return total[at : at + 2]

        back_rows = [[listed(0, 0)], [listed(1, 0)]]
        back_own = []
        for u in range(1, U):
            message = jnp.concatenate([listed(t, u) for t in range(3)], axis=0)
            got = lax.ppermute(message, "cols", col_perm[u - 1])
            if u == 1:
                own, local_send = local_scatter()
                got, local_send = lax.optimization_barrier((got, local_send))
                recv = lax.ppermute(local_send, "sub", sub_perm)
            back_rows[0].append(got[0:2])
            back_rows[1].append(got[2:4])
            back_own.append(got[4:6])
        returns = [
            lax.ppermute(jnp.concatenate(x, axis=0), "rows", perm)
            for x, perm in zip(back_rows, row_perm)
        ] + [jnp.concatenate(back_own, axis=0)]
        last = step == STEPS - 1
        outs = pl.pallas_call(
            functools.partial(update_kernel, 3, last),
            out_shape=[f32_out(6, 2048)] * 2 if last else [f32_out(16, 8, 128), f32_out(6, 2048)] + list_outs,
            in_specs=[VMEM] * 9,
            out_specs=[VMEM] * (2 if last else 5),
            scratch_shapes=[pltpu.VMEM((128, 256 * n), BF16), pltpu.VMEM((256, 256 * n), BF16)],
            compiler_params=params(),
        )(own, recv, field, speed, mass, picks, *returns)
        field, speed = outs[:2]
        outgoing = outs[2:]
    return field, speed


def solution(mesh):
    whole = ("groups", "rows", "cols", "sub")
    in_specs = (
        P(None, whole),
        P(None, whole),
        P(whole),
        P("rows", "cols", ("groups", "sub")),
        P(None, whole),
        P(None, whole),
        P(whole),
        P(whole),
        P(),
    )
    out_specs = (P(None, whole), P(None, whole))
    return jax.shard_map(shards, mesh=mesh, in_specs=in_specs, out_specs=out_specs, check_vma=False)
```

```python
import functools

import jax
import jax.numpy as jnp
from jax import lax
from jax.experimental import pallas as pl
from jax.experimental.pallas import tpu as pltpu
from jax.sharding import PartitionSpec as P

STEPS = 2
F32 = jnp.float32
BF16 = jnp.bfloat16
VMEM = pl.BlockSpec(memory_space=pltpu.VMEM)


def lane_pick(row, lanes):
    return jnp.take_along_axis(row, lanes, axis=1, mode="promise_in_bounds")


def spread(row):
    return jnp.broadcast_to(row, (8, 128))


def split(value):
    high = value.astype(BF16).astype(F32)
    return high, value - high


def padded(tile):
    return jnp.concatenate([tile, jnp.zeros((8 - tile.shape[0], 128), F32)], axis=0)


def pick_lists(field_ref, picks_ref, outs):
    picks = [picks_ref[0:8, :], picks_ref[8:16, :]]
    lanes = [p & 127 for p in picks]
    rows = [lax.shift_right_logical(p, 7) for p in picks]
    found = [[jnp.zeros((8, 128), F32) for _ in range(2)] for _ in range(6)]
    for tile in range(16):
        hit = [r == tile for r in rows]
        for c in range(6):
            row = spread(field_ref[tile, c : c + 1, :])
            for v in range(2):
                found[c][v] = jnp.where(hit[v], lane_pick(row, lanes[v]), found[c][v])
    for c in range(8):
        both = jnp.concatenate(found[c], axis=0) if c < 6 else jnp.zeros((16, 128), F32)
        at = 0
        for out in outs:
            size = out.shape[0]
            out[:, c, :] = both[at : at + size, :]
            at += size


def lists_kernel(U, odd_ref, displace_ref, send_ref, field_ref, picks_ref, *outs):
    r_odd, c_odd = odd_ref[0:1, :], odd_ref[1:2, :]
    for half in range(2):
        lists = [send_ref[a][:, half * 128 : (half + 1) * 128] for a in range(3)]
        swap = [jnp.where(r_odd == 0, lists[2 * t], lists[2 - 2 * t]) for t in (1, 0)] + [lists[1]]
        at = half
        for t in range(3):
            ordered = [swap[t][1:2]]
            ordered += [
                jnp.where(c_odd == 0, swap[t][2 * u : 2 * u + 1], swap[t][2 - 2 * u : 3 - 2 * u]) for u in (1, 0)
            ]
            for u in range(U):
                if t < 2 or u > 0:
                    picks_ref[at : at + 1, :] = ordered[u]
                    at += 2
    at -= 1
    if at < 16:
        picks_ref[at:16, :] = jnp.zeros((16 - at, 128), jnp.int32)
    for tile in range(16):
        field_ref[tile] = padded(displace_ref[:, tile * 128 : (tile + 1) * 128])
    pick_lists(field_ref, picks_ref, outs)


def relative_slots(U, n, odd_ref, raw_ref, slots_ref):
    r_odd, c_odd, s = odd_ref[0:1, :], odd_ref[1:2, :], odd_ref[2:3, :]
    for tile in range(16):
        cols = slice(tile * 128, (tile + 1) * 128)
        raw = raw_ref[:, cols]
        hi = lax.shift_right_logical(raw, 8)
        sender = (hi >= 25).astype(jnp.int32)
        direction = hi - 16 - 9 * sender
        a = (direction >= 3).astype(jnp.int32) + (direction >= 6).astype(jnp.int32)
        b = direction - 3 * a
        a = jnp.where(r_odd == 0, a, 2 - a)
        b = jnp.where(c_odd == 0, b, 2 - b)
        t = jnp.where(a == 1, 2, jnp.where(a == 0, 0, 1))
        u = jnp.where(b == 1, 0, jnp.where(b == 0, 1, 2))
        order = jnp.where(t == 2, 2 * U + u - 1, t * U + u)
        near = jnp.where(u < U, 16 + n * jnp.where(sender == s, 0, 1) + order, 64)
        own = jnp.where(hi >= 8, hi - 8, hi) + 8 * jnp.where((hi >= 8).astype(jnp.int32) == s, 0, 1)
        slots_ref[:, cols] = jnp.where(hi < 16, own, near) * 256 + (raw & 255)


def one_hot(lanes):
    lanes = jnp.broadcast_to(lanes.astype(F32), (16, 128)).astype(BF16)
    iota = lax.broadcasted_iota(jnp.int32, (16, 128), 0).astype(F32)
    one, zero = jnp.ones((16, 128), BF16), jnp.zeros((16, 128), BF16)
    return jnp.concatenate(
        [jnp.where((iota + 16.0 * at).astype(BF16) == lanes, one, zero) for at in range(16)], axis=0
    )


def times_one_hot(values, hot):
    return lax.dot_general(values, hot, (((1,), (1,)), ((), ())), preferred_element_type=F32)


def build_hot(e, quad, slots_ref, hot_ref):
    for bb in range(4):
        b = quad * 4 + bb
        for k in range(3):
            slot = slots_ref[3 * e + k : 3 * e + k + 1, b * 128 : (b + 1) * 128]
            at = (e * 48 + b * 3 + k) * 128
            hot_ref[:, at : at + 128] = one_hot(slot & 255)


def fill_table(tiles, table_ref):
    low_at = len(tiles) * 8
    for row in range(0, len(tiles), 2):
        for half in range(2):
            both = jnp.concatenate([tiles[row](half), tiles[row + 1](half)], axis=0)
            for base, piece in zip((0, low_at), split(both)):
                table_ref[base + row * 8 : base + row * 8 + 16, half * 128 : (half + 1) * 128] = piece.astype(BF16)


def gather_step(e, quad, first, rows, table_ref, hot_ref, x_refs, slots_ref, shape_ref, vec_ref, base_ref=None):
    low_at = rows * 8
    start = (4 * e + quad) * 1536
    x_ref = x_refs.at[quad % 2]
    x_ref[...] = jnp.dot(table_ref[...], hot_ref[:, start : start + 1536], preferred_element_type=F32)
    for bb in range(4):
        b = quad * 4 + bb
        cols = slice(b * 128, (b + 1) * 128)
        end = jnp.zeros((8, 128), F32) if base_ref is None else base_ref[:, cols]
        for k in range(3):
            j = 3 * e + k
            hi = spread(lax.shift_right_logical(slots_ref[j : j + 1, cols], 8))
            at = (bb * 3 + k) * 128
            found = jnp.zeros((8, 128), F32)
            for row in range(rows):
                high = x_ref[row * 8 : row * 8 + 8, at : at + 128]
                low = x_ref[low_at + row * 8 : low_at + row * 8 + 8, at : at + 128]
                found = jnp.where(hi == first + row, high + low, found)
            end += found * spread(shape_ref[j : j + 1, cols])
        vec_ref[:, cols] = end


def scatter_step(e, quad, first, rows, force_ref, a_refs, acc_ref, hot_ref, slots_ref, shape_ref, weight_ref):
    low_at = rows * 8
    start = (4 * e + quad) * 1536
    a_ref = a_refs.at[quad % 2]
    for bb in range(4):
        b = quad * 4 + bb
        cols = slice(b * 128, (b + 1) * 128)
        force = force_ref[e * 8 : e * 8 + 8, cols]
        weight = weight_ref[b : b + 1, :]
        for k in range(3):
            j = 3 * e + k
            at = (bb * 3 + k) * 128
            hi = spread(lax.shift_right_logical(slots_ref[j : j + 1, cols], 8))
            pieces = split(force * spread(shape_ref[j : j + 1, cols] * weight))
            for row in range(0, rows, 2):
                hit = [hi == first + row, hi == first + row + 1]
                for base, piece in zip((0, low_at), pieces):
                    a_ref[base + row * 8 : base + row * 8 + 16, at : at + 128] = jnp.concatenate(
                        [jnp.where(hit[0], piece, 0.0), jnp.where(hit[1], piece, 0.0)], axis=0
                    ).astype(BF16)
    acc_ref[...] += times_one_hot(a_ref[...], hot_ref[:, start : start + 1536])


def first_gather_kernel(relate, field_ref, other_ref, odd_ref, raw_ref, shape_ref, slots_ref, *refs):
    relate(odd_ref, raw_ref, slots_ref)
    local_gather_kernel(0, True, field_ref, other_ref, slots_ref, shape_ref, *refs)


def second_gather_kernel(kinds, field_ref, other_ref, slots_ref, shape_ref, stiff_ref, vec_ref, spread_ref, *refs):
    spread_ref[...] = spread_stiffness(kinds, stiff_ref[...])
    local_gather_kernel(1, True, field_ref, other_ref, slots_ref, shape_ref, vec_ref, *refs)


def local_gather_kernel(e, build, *refs):
    if build:
        field_ref, other_ref, slots_ref, shape_ref, vec_ref, table_ref, x_refs, hot_ref = refs
    else:
        field_ref, other_ref, slots_ref, shape_ref, hot_ref, vec_ref, table_ref, x_refs = refs
    tiles = [lambda half, k=k: field_ref[2 * k + half] for k in range(8)]
    tiles += [lambda half, k=k: other_ref[2 * k + half] for k in range(8)]
    fill_table(tiles, table_ref)
    for quad in range(4):
        if build:
            build_hot(e, quad, slots_ref, hot_ref)
        gather_step(e, quad, 0, 16, table_ref, hot_ref, x_refs, slots_ref, shape_ref, vec_ref)


def spread_stiffness(kinds, flat):
    rows = lax.broadcasted_iota(jnp.int32, (16 * kinds, 12 * kinds), 0)
    cols = lax.broadcasted_iota(jnp.int32, (16 * kinds, 12 * kinds), 1)
    within = rows & 15
    component = within & 7
    source = jnp.where(within >= 8, 6 + component, component) * kinds + lax.shift_right_logical(rows, 4)
    pick = jnp.where((component < 6) & (cols == source), 1.0, 0.0)
    place_row = lax.broadcasted_iota(jnp.int32, (12, 96), 0)
    within = lax.broadcasted_iota(jnp.int32, (12, 96), 1) & 15
    component = within & 7
    place = jnp.where((component < 6) & (place_row == jnp.where(within >= 8, 6 + component, component)), 1.0, 0.0)
    high = lax.Precision.HIGHEST
    taken = jnp.dot(pick, flat, precision=high, preferred_element_type=F32)
    return jnp.dot(taken, place, precision=high, preferred_element_type=F32)


def near_kernel(n, kinds, build, *refs):
    vec0_ref, vec1_ref, near_ref, other_ref, slots_ref, shape_ref, kind_ref, weight_ref, stiff_ref = refs[:9]
    if build:
        own_near_ref, send_ref, force_ref, hot_ref, *refs = refs[9:]
    else:
        hot_ref, own_near_ref, send_ref, force_ref, *refs = refs[9:]
    table_ref, x_refs, vec_ref, cat_ref, kinds_ref, a_refs, acc_ref = refs
    tiles = [lambda half, k=k: near_ref[2 * k + half] for k in range(n)]
    tiles += [lambda half, k=k: other_ref[2 * k + half] for k in range(n)]
    fill_table(tiles, table_ref)
    for e, base_ref in enumerate((vec0_ref, vec1_ref)):
        for quad in range(4):
            if build:
                build_hot(e, quad, slots_ref, hot_ref)
            gather_step(
                e, quad, 16, 2 * n, table_ref, hot_ref, x_refs, slots_ref, shape_ref, vec_ref.at[e], base_ref
            )

    v1, rest = split(jnp.concatenate([vec_ref[0], vec_ref[1]], axis=0))
    v2, v3 = split(rest)
    for at, piece in enumerate((v1, v2, v1, v2, v3, v1)):
        cat_ref[at * 16 : (at + 1) * 16, :] = piece.astype(BF16)
    s1, rest = split(stiff_ref[...])
    s2, s3 = split(rest)
    block = lax.broadcasted_iota(jnp.int32, s1.shape, 1) // 16
    stiff = jnp.where((block == 2) | (block == 3), s2, jnp.where(block == 5, s3, s1)).astype(BF16)
    kinds_ref[...] = jnp.dot(stiff, cat_ref[...], preferred_element_type=F32)
    for b in range(16):
        cols = slice(b * 128, (b + 1) * 128)
        kind = spread(kind_ref[b : b + 1, :])
        for e in range(2):
            force = jnp.zeros((8, 128), F32)
            for t in range(kinds):
                force = jnp.where(kind == t, kinds_ref[t * 16 + e * 8 : t * 16 + e * 8 + 8, cols], force)
            force_ref[e * 8 : (e + 1) * 8, cols] = force

    acc_ref[...] = jnp.zeros_like(acc_ref)
    for e in range(2):
        for quad in range(4):
            scatter_step(e, quad, 16, 2 * n, force_ref, a_refs, acc_ref, hot_ref, slots_ref, shape_ref, weight_ref)
    for row in range(2 * n):
        total = acc_ref[row * 8 : row * 8 + 8, :] + acc_ref[(2 * n + row) * 8 : (2 * n + row) * 8 + 8, :]
        for half in range(2):
            out, at = (own_near_ref, row) if row < n else (send_ref, row - n)
            out[2 * at + half] = total[:, half * 128 : (half + 1) * 128]


def local_scatter_kernel(force_ref, hot_ref, slots_ref, shape_ref, weight_ref, own_ref, send_ref, a_refs, acc_ref):
    acc_ref[...] = jnp.zeros_like(acc_ref)
    for e in range(2):
        for quad in range(4):
            scatter_step(e, quad, 0, 16, force_ref, a_refs, acc_ref, hot_ref, slots_ref, shape_ref, weight_ref)
    for row in range(16):
        total = acc_ref[row * 8 : row * 8 + 8, :] + acc_ref[128 + row * 8 : 128 + row * 8 + 8, :]
        for half in range(2):
            out, at = (own_ref, row) if row < 8 else (send_ref, row - 8)
            out[2 * at + half] = total[:, half * 128 : (half + 1) * 128]


def update_kernel(n_returns, last, own_ref, recv_ref, field_ref, velocity_ref, mass_ref, picks_ref, *refs):
    returns, refs = refs[:n_returns], refs[n_returns:]
    new_field_ref, new_velocity_ref = refs[0], refs[1]
    a_ref, b_ref = refs[-2], refs[-1]
    outs = refs[2:-2]
    p = 0
    for ret in returns:
        for tile in range(ret.shape[0]):
            pick = picks_ref[p : p + 1, :]
            hi = spread(lax.shift_right_logical(pick, 8))
            at = p * 128
            for base, piece in zip((0, 64), split(ret[tile])):
                a_ref[base : base + 64, at : at + 128] = jnp.concatenate(
                    [jnp.where(hi == row, piece, 0.0) for row in range(8)], axis=0
                ).astype(BF16)
            b_ref[:, at : at + 128] = one_hot(pick & 255)
            p += 1
    back = times_one_hot(a_ref[...], b_ref[...])
    back = back[:64] + back[64:]
    for tile in range(16):
        row, half = tile // 2, tile % 2
        cols = slice(tile * 128, (tile + 1) * 128)
        force = own_ref[tile] + recv_ref[tile] + back[row * 8 : row * 8 + 8, half * 128 : (half + 1) * 128]
        velocity = 0.98 * velocity_ref[:, cols] - 0.2 * force[0:6] / mass_ref[:, cols]
        new_velocity_ref[:, cols] = velocity
        field = field_ref[tile][0:6] + 0.2 * velocity
        if last:
            new_field_ref[:, cols] = field
        else:
            new_field_ref[tile] = padded(field)
    if not last:
        pick_lists(new_field_ref, picks_ref, outs)


def pairs(count, shift):
    out = []
    for i in range(shift, count - 1, 2):
        out += [(i, i + 1), (i + 1, i)]
    return out


def f32_out(*shape):
    return jax.ShapeDtypeStruct(shape, F32)


def params():
    return pltpu.CompilerParams(vmem_limit_bytes=24 * 1024 * 1024)


def cost(us):
    return pl.CostEstimate(flops=us * 10**9, bytes_accessed=us * 10**6, transcendentals=0)


def shards(
    displace,
    velocity,
    nodal_mass,
    send_list,
    beam_slots,
    shape_values,
    beam_kind,
    cluster_weight,
    stiffness,
):
    list_len = send_list.shape[2]
    cols = lax.axis_size("cols")
    U = 2 if cols <= 2 else 3
    n = 3 * U - 1
    kinds = stiffness.shape[0]
    r_odd = lax.axis_index("rows") % 2
    c_odd = lax.axis_index("cols") % 2
    s = lax.axis_index("sub")
    row_perm = [pairs(lax.axis_size("rows"), 0), pairs(lax.axis_size("rows"), 1)]
    col_perm = [pairs(cols, 0), pairs(cols, 1)][: U - 1]
    cross_perm = [[(2 * a + k, 2 * b + 1 - k) for a, b in perm for k in range(2)] for perm in col_perm]
    sub_perm = [(0, 1), (1, 0)]

    kind = beam_kind.reshape(16, 128)
    weight = cluster_weight.reshape(16, 128)
    stiff = stiffness.transpose(1, 0, 2).reshape(12 * kinds, 12)
    mass = nodal_mass.reshape(1, -1)

    speed = velocity
    list_outs = [f32_out(2 * U, 8, 128), f32_out(2 * U, 8, 128), f32_out(2 * U - 2, 8, 128)]
    odd = jnp.broadcast_to(jnp.stack([r_odd, c_odd, s]).astype(jnp.int32)[:, None], (3, 128))
    field, picks, *outgoing = pl.pallas_call(
        functools.partial(lists_kernel, U),
        out_shape=[f32_out(16, 8, 128), jax.ShapeDtypeStruct((16, 128), jnp.int32)] + list_outs,
        in_specs=[VMEM] * 3,
        out_specs=[VMEM] * 5,
        compiler_params=params(),
    )(odd, displace, send_list)
    hot = None
    tall = 32 * n
    for step in range(STEPS):
        other = lax.ppermute(field, "sub", sub_perm)
        build = hot is None

        def local_gather(kernel, out_shape, specs, *operands):
            return pl.pallas_call(
                kernel,
                out_shape=out_shape,
                in_specs=specs,
                out_specs=[VMEM] * len(out_shape),
                scratch_shapes=[pltpu.VMEM((256, 256), BF16), pltpu.VMEM((2, 256, 1536), F32)]
                + ([pltpu.VMEM((256, 12288), BF16)] if build else []),
                compiler_params=params(),
                cost_estimate=cost(2),
            )(field, *operands)

        def plain(e, other):
            kernel = functools.partial(local_gather_kernel, e, False)
            return local_gather(kernel, [f32_out(8, 2048)], [VMEM] * 5, other, slots, shape_values, hot)[0]

        to_rows, own_row = outgoing[:2], outgoing[2]
        arrived = [lax.ppermute(x, "rows", perm) for x, perm in zip(to_rows, row_perm)]
        if build:
            slots, vec0 = local_gather(
                functools.partial(first_gather_kernel, functools.partial(relative_slots, U, n)),
                [jax.ShapeDtypeStruct((6, 2048), jnp.int32), f32_out(8, 2048)],
                [VMEM] * 5,
                other,
                odd,
                beam_slots,
                shape_values,
            )
        else:
            vec0 = plain(0, other)
        arrived[0], arrived[1], vec0, other = lax.optimization_barrier((arrived[0], arrived[1], vec0, other))
        direct = jnp.concatenate([arrived[0][0:2], arrived[1][0:2]], axis=0)
        direct_other = lax.ppermute(direct, "sub", sub_perm)
        near = [[direct[0:2]], [direct[2:4]], []]
        near_other = [[direct_other[0:2]], [direct_other[2:4]], []]
        for u in range(1, U):
            at = 2 * u
            message = jnp.concatenate(
                [arrived[0][at : at + 2], arrived[1][at : at + 2], own_row[at - 2 : at]], axis=0
            )
            got = lax.ppermute(message, "cols", col_perm[u - 1])
            crossed = lax.ppermute(message, ("cols", "sub"), cross_perm[u - 1])
            for t in range(3):
                near[t].append(got[2 * t : 2 * t + 2])
                near_other[t].append(crossed[2 * t : 2 * t + 2])
        near = jnp.concatenate(near[0] + near[1] + near[2], axis=0)
        near_other = jnp.concatenate(near_other[0] + near_other[1] + near_other[2], axis=0)
        if build:
            vec1, stiff = local_gather(
                functools.partial(second_gather_kernel, kinds),
                [f32_out(8, 2048), f32_out(16 * kinds, 96)],
                [VMEM] * 5,
                other,
                slots,
                shape_values,
                stiff,
            )
        else:
            vec1 = plain(1, other)
        own_near, near_send, force, *made = pl.pallas_call(
            functools.partial(near_kernel, n, kinds, build),
            out_shape=[f32_out(2 * n, 8, 128), f32_out(2 * n, 8, 128), f32_out(16, 2048)]
            + ([jax.ShapeDtypeStruct((256, 12288), BF16)] if build else []),
            in_specs=[VMEM] * (9 if build else 10),
            out_specs=[VMEM] * (4 if build else 3),
            scratch_shapes=[
                pltpu.VMEM((tall, 256), BF16),
                pltpu.VMEM((2, tall, 1536), F32),
                pltpu.VMEM((2, 8, 2048), F32),
                pltpu.VMEM((96, 2048), BF16),
                pltpu.VMEM((16 * kinds, 2048), F32),
                pltpu.VMEM((2, tall, 1536), BF16),
                pltpu.VMEM((tall, 256), F32),
            ],
            compiler_params=params(),
            cost_estimate=cost(5),
        )(vec0, vec1, near, near_other, slots, shape_values, kind, weight, stiff, *([] if build else [hot]))
        hot = made[0] if build else hot

        def local_scatter():
            return pl.pallas_call(
                local_scatter_kernel,
                out_shape=[f32_out(16, 8, 128)] * 2,
                in_specs=[VMEM] * 5,
                out_specs=[VMEM] * 2,
                scratch_shapes=[pltpu.VMEM((2, 256, 1536), BF16), pltpu.VMEM((256, 256), F32)],
                compiler_params=params(),
                cost_estimate=cost(3),
            )(force, hot, slots, shape_values, weight)

        def listed(x, t, u):
            at = 2 * (t * U + u) if t < 2 else 2 * (2 * U + u - 1)
            return x[at : at + 2]

        direct = jnp.concatenate([listed(near_send, 0, 0), listed(near_send, 1, 0)], axis=0)
        direct = lax.ppermute(direct, "sub", sub_perm)
        back_rows = [[listed(own_near, t, 0) + direct[2 * t : 2 * t + 2]] for t in range(2)]
        back_own = []
        for u in range(1, U):
            messages = [
                jnp.concatenate([listed(x, t, u) for t in range(3)], axis=0) for x in (own_near, near_send)
            ]
            got = lax.ppermute(messages[0], "cols", col_perm[u - 1])
            got += lax.ppermute(messages[1], ("cols", "sub"), cross_perm[u - 1])
            if u == 1:
                own, local_send = local_scatter()
                got, local_send = lax.optimization_barrier((got, local_send))
                recv = lax.ppermute(local_send, "sub", sub_perm)
            back_rows[0].append(got[0:2])
            back_rows[1].append(got[2:4])
            back_own.append(got[4:6])
        returns = [
            lax.ppermute(jnp.concatenate(x, axis=0), "rows", perm)
            for x, perm in zip(back_rows, row_perm)
        ] + [jnp.concatenate(back_own, axis=0)]
        last = step == STEPS - 1
        outs = pl.pallas_call(
            functools.partial(update_kernel, 3, last),
            out_shape=[f32_out(6, 2048)] * 2 if last else [f32_out(16, 8, 128), f32_out(6, 2048)] + list_outs,
            in_specs=[VMEM] * 9,
            out_specs=[VMEM] * (2 if last else 5),
            scratch_shapes=[pltpu.VMEM((128, 256 * n), BF16), pltpu.VMEM((256, 256 * n), BF16)],
            compiler_params=params(),
        )(own, recv, field, speed, mass, picks, *returns)
        field, speed = outs[:2]
        outgoing = outs[2:]
    return field, speed


def solution(mesh):
    whole = ("groups", "rows", "cols", "sub")
    in_specs = (
        P(None, whole),
        P(None, whole),
        P(whole),
        P("rows", "cols", ("groups", "sub")),
        P(None, whole),
        P(None, whole),
        P(whole),
        P(whole),
        P(),
    )
    out_specs = (P(None, whole), P(None, whole))
    return jax.shard_map(shards, mesh=mesh, in_specs=in_specs, out_specs=out_specs, check_vma=False)
```

```python
import functools

import jax
import jax.numpy as jnp
from jax import lax
from jax.experimental import pallas as pl
from jax.experimental.pallas import tpu as pltpu
from jax.sharding import PartitionSpec as P

STEPS = 2
F32 = jnp.float32
BF16 = jnp.bfloat16
VMEM = pl.BlockSpec(memory_space=pltpu.VMEM)


def lane_pick(row, lanes):
    return jnp.take_along_axis(row, lanes, axis=1, mode="promise_in_bounds")


def spread(row):
    return jnp.broadcast_to(row, (8, 128))


def split(value):
    high = value.astype(BF16).astype(F32)
    return high, value - high


def padded(tile):
    return jnp.concatenate([tile, jnp.zeros((8 - tile.shape[0], 128), F32)], axis=0)


def pick_lists(field_ref, picks_ref, outs):
    picks = [picks_ref[0:8, :], picks_ref[8:16, :]]
    lanes = [p & 127 for p in picks]
    rows = [lax.shift_right_logical(p, 7) for p in picks]
    found = [[jnp.zeros((8, 128), F32) for _ in range(2)] for _ in range(6)]
    for tile in range(16):
        hit = [r == tile for r in rows]
        for c in range(6):
            row = spread(field_ref[tile, c : c + 1, :])
            for v in range(2):
                found[c][v] = jnp.where(hit[v], lane_pick(row, lanes[v]), found[c][v])
    for c in range(8):
        both = jnp.concatenate(found[c], axis=0) if c < 6 else jnp.zeros((16, 128), F32)
        at = 0
        for out in outs:
            size = out.shape[0]
            out[:, c, :] = both[at : at + size, :]
            at += size


def lists_kernel(U, odd_ref, displace_ref, send_ref, field_ref, picks_ref, *outs):
    r_odd, c_odd = odd_ref[0:1, :], odd_ref[1:2, :]
    for half in range(2):
        lists = [send_ref[a][:, half * 128 : (half + 1) * 128] for a in range(3)]
        swap = [jnp.where(r_odd == 0, lists[2 * t], lists[2 - 2 * t]) for t in (1, 0)] + [lists[1]]
        at = half
        for t in range(3):
            ordered = [swap[t][1:2]]
            ordered += [
                jnp.where(c_odd == 0, swap[t][2 * u : 2 * u + 1], swap[t][2 - 2 * u : 3 - 2 * u]) for u in (1, 0)
            ]
            for u in range(U):
                if t < 2 or u > 0:
                    picks_ref[at : at + 1, :] = ordered[u]
                    at += 2
    at -= 1
    if at < 16:
        picks_ref[at:16, :] = jnp.zeros((16 - at, 128), jnp.int32)
    for tile in range(16):
        field_ref[tile] = padded(displace_ref[:, tile * 128 : (tile + 1) * 128])
    pick_lists(field_ref, picks_ref, outs)


def relative_slots(U, n, odd_ref, raw_ref, slots_ref):
    r_odd, c_odd, s = odd_ref[0:1, :], odd_ref[1:2, :], odd_ref[2:3, :]
    for tile in range(16):
        cols = slice(tile * 128, (tile + 1) * 128)
        raw = raw_ref[:, cols]
        hi = lax.shift_right_logical(raw, 8)
        sender = (hi >= 25).astype(jnp.int32)
        direction = hi - 16 - 9 * sender
        a = (direction >= 3).astype(jnp.int32) + (direction >= 6).astype(jnp.int32)
        b = direction - 3 * a
        a = jnp.where(r_odd == 0, a, 2 - a)
        b = jnp.where(c_odd == 0, b, 2 - b)
        t = jnp.where(a == 1, 2, jnp.where(a == 0, 0, 1))
        u = jnp.where(b == 1, 0, jnp.where(b == 0, 1, 2))
        order = jnp.where(t == 2, 2 * U + u - 1, t * U + u)
        near = jnp.where(u < U, 16 + n * jnp.where(sender == s, 0, 1) + order, 64)
        own = jnp.where(hi >= 8, hi - 8, hi) + 8 * jnp.where((hi >= 8).astype(jnp.int32) == s, 0, 1)
        slots_ref[:, cols] = jnp.where(hi < 16, own, near) * 256 + (raw & 255)


def one_hot(lanes):
    lanes = jnp.broadcast_to(lanes.astype(F32), (16, 128)).astype(BF16)
    iota = lax.broadcasted_iota(jnp.int32, (16, 128), 0).astype(F32)
    one, zero = jnp.ones((16, 128), BF16), jnp.zeros((16, 128), BF16)
    return jnp.concatenate(
        [jnp.where((iota + 16.0 * at).astype(BF16) == lanes, one, zero) for at in range(16)], axis=0
    )


def times_one_hot(values, hot):
    return lax.dot_general(values, hot, (((1,), (1,)), ((), ())), preferred_element_type=F32)


def build_hot(e, quad, slots_ref, hot_ref):
    for bb in range(4):
        b = quad * 4 + bb
        for k in range(3):
            slot = slots_ref[3 * e + k : 3 * e + k + 1, b * 128 : (b + 1) * 128]
            at = (e * 48 + b * 3 + k) * 128
            hot_ref[:, at : at + 128] = one_hot(slot & 255)


def fill_table(tiles, table_ref):
    low_at = len(tiles) * 8
    for row in range(0, len(tiles), 2):
        for half in range(2):
            both = jnp.concatenate([tiles[row](half), tiles[row + 1](half)], axis=0)
            for base, piece in zip((0, low_at), split(both)):
                table_ref[base + row * 8 : base + row * 8 + 16, half * 128 : (half + 1) * 128] = piece.astype(BF16)


def gather_step(e, quad, first, rows, table_ref, hot_ref, x_refs, slots_ref, shape_ref, vec_ref, base_ref=None):
    low_at = rows * 8
    start = (4 * e + quad) * 1536
    x_ref = x_refs.at[quad % 2]
    x_ref[...] = jnp.dot(table_ref[...], hot_ref[:, start : start + 1536], preferred_element_type=F32)
    for bb in range(4):
        b = quad * 4 + bb
        cols = slice(b * 128, (b + 1) * 128)
        end = jnp.zeros((8, 128), F32) if base_ref is None else base_ref[:, cols]
        for k in range(3):
            j = 3 * e + k
            hi = spread(lax.shift_right_logical(slots_ref[j : j + 1, cols], 8))
            at = (bb * 3 + k) * 128
            found = jnp.zeros((8, 128), F32)
            for row in range(rows):
                high = x_ref[row * 8 : row * 8 + 8, at : at + 128]
                low = x_ref[low_at + row * 8 : low_at + row * 8 + 8, at : at + 128]
                found = jnp.where(hi == first + row, high + low, found)
            end += found * spread(shape_ref[j : j + 1, cols])
        vec_ref[:, cols] = end


def scatter_step(e, quad, first, rows, force_ref, a_refs, acc_ref, hot_ref, slots_ref, shape_ref, weight_ref):
    low_at = rows * 8
    start = (4 * e + quad) * 1536
    a_ref = a_refs.at[quad % 2]
    for bb in range(4):
        b = quad * 4 + bb
        cols = slice(b * 128, (b + 1) * 128)
        force = force_ref[e * 8 : e * 8 + 8, cols]
        weight = weight_ref[b : b + 1, :]
        for k in range(3):
            j = 3 * e + k
            at = (bb * 3 + k) * 128
            hi = spread(lax.shift_right_logical(slots_ref[j : j + 1, cols], 8))
            pieces = split(force * spread(shape_ref[j : j + 1, cols] * weight))
            for row in range(0, rows, 2):
                hit = [hi == first + row, hi == first + row + 1]
                for base, piece in zip((0, low_at), pieces):
                    a_ref[base + row * 8 : base + row * 8 + 16, at : at + 128] = jnp.concatenate(
                        [jnp.where(hit[0], piece, 0.0), jnp.where(hit[1], piece, 0.0)], axis=0
                    ).astype(BF16)
    acc_ref[...] += times_one_hot(a_ref[...], hot_ref[:, start : start + 1536])


def first_gather_kernel(relate, field_ref, other_ref, odd_ref, raw_ref, shape_ref, slots_ref, *refs):
    relate(odd_ref, raw_ref, slots_ref)
    local_gather_kernel(0, True, field_ref, other_ref, slots_ref, shape_ref, *refs)


def second_gather_kernel(kinds, field_ref, other_ref, slots_ref, shape_ref, stiff_ref, vec_ref, spread_ref, hot_ref, *refs):
    spread_ref[...] = spread_stiffness(kinds, stiff_ref[...])
    for quad in range(4):
        build_hot(0, quad, slots_ref, hot_ref)
    local_gather_kernel(1, True, field_ref, other_ref, slots_ref, shape_ref, vec_ref, *refs, hot_ref)


def local_gather_kernel(e, build, *refs):
    if build:
        field_ref, other_ref, slots_ref, shape_ref, vec_ref, table_ref, x_refs, hot_ref = refs
    else:
        field_ref, other_ref, slots_ref, shape_ref, hot_ref, vec_ref, table_ref, x_refs = refs
    tiles = [lambda half, k=k: field_ref[2 * k + half] for k in range(8)]
    tiles += [lambda half, k=k: other_ref[2 * k + half] for k in range(8)]
    fill_table(tiles, table_ref)
    for quad in range(4):
        if build:
            build_hot(e, quad, slots_ref, hot_ref)
        gather_step(e, quad, 0, 16, table_ref, hot_ref, x_refs, slots_ref, shape_ref, vec_ref)


def spread_stiffness(kinds, flat):
    rows = lax.broadcasted_iota(jnp.int32, (16 * kinds, 12 * kinds), 0)
    cols = lax.broadcasted_iota(jnp.int32, (16 * kinds, 12 * kinds), 1)
    within = rows & 15
    component = within & 7
    source = jnp.where(within >= 8, 6 + component, component) * kinds + lax.shift_right_logical(rows, 4)
    pick = jnp.where((component < 6) & (cols == source), 1.0, 0.0)
    place_row = lax.broadcasted_iota(jnp.int32, (12, 96), 0)
    within = lax.broadcasted_iota(jnp.int32, (12, 96), 1) & 15
    component = within & 7
    place = jnp.where((component < 6) & (place_row == jnp.where(within >= 8, 6 + component, component)), 1.0, 0.0)
    high = lax.Precision.HIGHEST
    taken = jnp.dot(pick, flat, precision=high, preferred_element_type=F32)
    return jnp.dot(taken, place, precision=high, preferred_element_type=F32)


def near_kernel(n, kinds, *refs):
    vec0_ref, vec1_ref, near_ref, other_ref, slots_ref, shape_ref, kind_ref, weight_ref, stiff_ref = refs[:9]
    hot_ref, own_near_ref, send_ref, force_ref, *refs = refs[9:]
    table_ref, x_refs, vec_ref, cat_ref, kinds_ref, a_refs, acc_ref = refs
    tiles = [lambda half, k=k: near_ref[2 * k + half] for k in range(n)]
    tiles += [lambda half, k=k: other_ref[2 * k + half] for k in range(n)]
    fill_table(tiles, table_ref)
    for e, base_ref in enumerate((vec0_ref, vec1_ref)):
        for quad in range(4):
            gather_step(
                e, quad, 16, 2 * n, table_ref, hot_ref, x_refs, slots_ref, shape_ref, vec_ref.at[e], base_ref
            )

    v1, rest = split(jnp.concatenate([vec_ref[0], vec_ref[1]], axis=0))
    v2, v3 = split(rest)
    for at, piece in enumerate((v1, v2, v1, v2, v3, v1)):
        cat_ref[at * 16 : (at + 1) * 16, :] = piece.astype(BF16)
    s1, rest = split(stiff_ref[...])
    s2, s3 = split(rest)
    block = lax.broadcasted_iota(jnp.int32, s1.shape, 1) // 16
    stiff = jnp.where((block == 2) | (block == 3), s2, jnp.where(block == 5, s3, s1)).astype(BF16)
    kinds_ref[...] = jnp.dot(stiff, cat_ref[...], preferred_element_type=F32)
    for b in range(16):
        cols = slice(b * 128, (b + 1) * 128)
        kind = spread(kind_ref[b : b + 1, :])
        for e in range(2):
            force = jnp.zeros((8, 128), F32)
            for t in range(kinds):
                force = jnp.where(kind == t, kinds_ref[t * 16 + e * 8 : t * 16 + e * 8 + 8, cols], force)
            force_ref[e * 8 : (e + 1) * 8, cols] = force

    acc_ref[...] = jnp.zeros_like(acc_ref)
    for e in range(2):
        for quad in range(4):
            scatter_step(e, quad, 16, 2 * n, force_ref, a_refs, acc_ref, hot_ref, slots_ref, shape_ref, weight_ref)
    for row in range(2 * n):
        total = acc_ref[row * 8 : row * 8 + 8, :] + acc_ref[(2 * n + row) * 8 : (2 * n + row) * 8 + 8, :]
        for half in range(2):
            out, at = (own_near_ref, row) if row < n else (send_ref, row - n)
            out[2 * at + half] = total[:, half * 128 : (half + 1) * 128]


def local_scatter_kernel(force_ref, hot_ref, slots_ref, shape_ref, weight_ref, own_ref, send_ref, a_refs, acc_ref):
    acc_ref[...] = jnp.zeros_like(acc_ref)
    for e in range(2):
        for quad in range(4):
            scatter_step(e, quad, 0, 16, force_ref, a_refs, acc_ref, hot_ref, slots_ref, shape_ref, weight_ref)
    for row in range(16):
        total = acc_ref[row * 8 : row * 8 + 8, :] + acc_ref[128 + row * 8 : 128 + row * 8 + 8, :]
        for half in range(2):
            out, at = (own_ref, row) if row < 8 else (send_ref, row - 8)
            out[2 * at + half] = total[:, half * 128 : (half + 1) * 128]


def update_kernel(n_returns, last, own_ref, recv_ref, field_ref, velocity_ref, mass_ref, picks_ref, *refs):
    returns, refs = refs[:n_returns], refs[n_returns:]
    new_field_ref, new_velocity_ref = refs[0], refs[1]
    a_ref, b_ref = refs[-2], refs[-1]
    outs = refs[2:-2]
    p = 0
    for ret in returns:
        for tile in range(ret.shape[0]):
            pick = picks_ref[p : p + 1, :]
            hi = spread(lax.shift_right_logical(pick, 8))
            at = p * 128
            for base, piece in zip((0, 64), split(ret[tile])):
                a_ref[base : base + 64, at : at + 128] = jnp.concatenate(
                    [jnp.where(hi == row, piece, 0.0) for row in range(8)], axis=0
                ).astype(BF16)
            b_ref[:, at : at + 128] = one_hot(pick & 255)
            p += 1
    back = times_one_hot(a_ref[...], b_ref[...])
    back = back[:64] + back[64:]
    for tile in range(16):
        row, half = tile // 2, tile % 2
        cols = slice(tile * 128, (tile + 1) * 128)
        force = own_ref[tile] + recv_ref[tile] + back[row * 8 : row * 8 + 8, half * 128 : (half + 1) * 128]
        velocity = 0.98 * velocity_ref[:, cols] - 0.2 * force[0:6] / mass_ref[:, cols]
        new_velocity_ref[:, cols] = velocity
        field = field_ref[tile][0:6] + 0.2 * velocity
        if last:
            new_field_ref[:, cols] = field
        else:
            new_field_ref[tile] = padded(field)
    if not last:
        pick_lists(new_field_ref, picks_ref, outs)


def pairs(count, shift):
    out = []
    for i in range(shift, count - 1, 2):
        out += [(i, i + 1), (i + 1, i)]
    return out


def f32_out(*shape):
    return jax.ShapeDtypeStruct(shape, F32)


def params():
    return pltpu.CompilerParams(vmem_limit_bytes=24 * 1024 * 1024)


def cost(us):
    return pl.CostEstimate(flops=us * 10**9, bytes_accessed=us * 10**6, transcendentals=0)


def shards(
    displace,
    velocity,
    nodal_mass,
    send_list,
    beam_slots,
    shape_values,
    beam_kind,
    cluster_weight,
    stiffness,
):
    list_len = send_list.shape[2]
    cols = lax.axis_size("cols")
    U = 2 if cols <= 2 else 3
    n = 3 * U - 1
    kinds = stiffness.shape[0]
    r_odd = lax.axis_index("rows") % 2
    c_odd = lax.axis_index("cols") % 2
    s = lax.axis_index("sub")
    row_perm = [pairs(lax.axis_size("rows"), 0), pairs(lax.axis_size("rows"), 1)]
    col_perm = [pairs(cols, 0), pairs(cols, 1)][: U - 1]
    cross_perm = [[(2 * a + k, 2 * b + 1 - k) for a, b in perm for k in range(2)] for perm in col_perm]
    sub_perm = [(0, 1), (1, 0)]

    kind = beam_kind.reshape(16, 128)
    weight = cluster_weight.reshape(16, 128)
    stiff = stiffness.transpose(1, 0, 2).reshape(12 * kinds, 12)
    mass = nodal_mass.reshape(1, -1)

    speed = velocity
    list_outs = [f32_out(2 * U, 8, 128), f32_out(2 * U, 8, 128), f32_out(2 * U - 2, 8, 128)]
    odd = jnp.broadcast_to(jnp.stack([r_odd, c_odd, s]).astype(jnp.int32)[:, None], (3, 128))
    field, picks, *outgoing = pl.pallas_call(
        functools.partial(lists_kernel, U),
        out_shape=[f32_out(16, 8, 128), jax.ShapeDtypeStruct((16, 128), jnp.int32)] + list_outs,
        in_specs=[VMEM] * 3,
        out_specs=[VMEM] * 5,
        compiler_params=params(),
    )(odd, displace, send_list)
    hot = None
    tall = 32 * n
    for step in range(STEPS):
        other = lax.ppermute(field, "sub", sub_perm)
        build = hot is None

        def local_gather(kernel, out_shape, specs, scratch, *operands):
            return pl.pallas_call(
                kernel,
                out_shape=out_shape,
                in_specs=specs,
                out_specs=[VMEM] * len(out_shape),
                scratch_shapes=[pltpu.VMEM((256, 256), BF16), pltpu.VMEM((2, 256, 1536), F32)]
                + scratch,
                compiler_params=params(),
                cost_estimate=cost(2),
            )(field, *operands)

        def plain(e, other):
            kernel = functools.partial(local_gather_kernel, e, False)
            return local_gather(kernel, [f32_out(8, 2048)], [VMEM] * 5, [], other, slots, shape_values, hot)[0]

        to_rows, own_row = outgoing[:2], outgoing[2]
        arrived = [lax.ppermute(x, "rows", perm) for x, perm in zip(to_rows, row_perm)]
        if build:
            slots, vec0 = local_gather(
                functools.partial(first_gather_kernel, functools.partial(relative_slots, U, n)),
                [jax.ShapeDtypeStruct((6, 2048), jnp.int32), f32_out(8, 2048)],
                [VMEM] * 5,
                [pltpu.VMEM((256, 12288), BF16)],
                other,
                odd,
                beam_slots,
                shape_values,
            )
        else:
            vec0 = plain(0, other)
        arrived[0], arrived[1], vec0, other = lax.optimization_barrier((arrived[0], arrived[1], vec0, other))
        direct = jnp.concatenate([arrived[0][0:2], arrived[1][0:2]], axis=0)
        direct_other = lax.ppermute(direct, "sub", sub_perm)
        near = [[direct[0:2]], [direct[2:4]], []]
        near_other = [[direct_other[0:2]], [direct_other[2:4]], []]
        for u in range(1, U):
            at = 2 * u
            message = jnp.concatenate(
                [arrived[0][at : at + 2], arrived[1][at : at + 2], own_row[at - 2 : at]], axis=0
            )
            got = lax.ppermute(message, "cols", col_perm[u - 1])
            crossed = lax.ppermute(message, ("cols", "sub"), cross_perm[u - 1])
            for t in range(3):
                near[t].append(got[2 * t : 2 * t + 2])
                near_other[t].append(crossed[2 * t : 2 * t + 2])
        near = jnp.concatenate(near[0] + near[1] + near[2], axis=0)
        near_other = jnp.concatenate(near_other[0] + near_other[1] + near_other[2], axis=0)
        if build:
            vec1, stiff, hot = local_gather(
                functools.partial(second_gather_kernel, kinds),
                [f32_out(8, 2048), f32_out(16 * kinds, 96), jax.ShapeDtypeStruct((256, 12288), BF16)],
                [VMEM] * 5,
                [],
                other,
                slots,
                shape_values,
                stiff,
            )
        else:
            vec1 = plain(1, other)
        own_near, near_send, force = pl.pallas_call(
            functools.partial(near_kernel, n, kinds),
            out_shape=[f32_out(2 * n, 8, 128), f32_out(2 * n, 8, 128), f32_out(16, 2048)],
            in_specs=[VMEM] * 10,
            out_specs=[VMEM] * 3,
            scratch_shapes=[
                pltpu.VMEM((tall, 256), BF16),
                pltpu.VMEM((2, tall, 1536), F32),
                pltpu.VMEM((2, 8, 2048), F32),
                pltpu.VMEM((96, 2048), BF16),
                pltpu.VMEM((16 * kinds, 2048), F32),
                pltpu.VMEM((2, tall, 1536), BF16),
                pltpu.VMEM((tall, 256), F32),
            ],
            compiler_params=params(),
            cost_estimate=cost(5),
        )(vec0, vec1, near, near_other, slots, shape_values, kind, weight, stiff, hot)

        def local_scatter():
            return pl.pallas_call(
                local_scatter_kernel,
                out_shape=[f32_out(16, 8, 128)] * 2,
                in_specs=[VMEM] * 5,
                out_specs=[VMEM] * 2,
                scratch_shapes=[pltpu.VMEM((2, 256, 1536), BF16), pltpu.VMEM((256, 256), F32)],
                compiler_params=params(),
                cost_estimate=cost(3),
            )(force, hot, slots, shape_values, weight)

        def listed(x, t, u):
            at = 2 * (t * U + u) if t < 2 else 2 * (2 * U + u - 1)
            return x[at : at + 2]

        direct = jnp.concatenate([listed(near_send, 0, 0), listed(near_send, 1, 0)], axis=0)
        direct = lax.ppermute(direct, "sub", sub_perm)
        back_rows = [[listed(own_near, t, 0) + direct[2 * t : 2 * t + 2]] for t in range(2)]
        back_own = []
        for u in range(1, U):
            messages = [
                jnp.concatenate([listed(x, t, u) for t in range(3)], axis=0) for x in (own_near, near_send)
            ]
            got = lax.ppermute(messages[0], "cols", col_perm[u - 1])
            got += lax.ppermute(messages[1], ("cols", "sub"), cross_perm[u - 1])
            if u == 1:
                own, local_send = local_scatter()
                got, local_send = lax.optimization_barrier((got, local_send))
                recv = lax.ppermute(local_send, "sub", sub_perm)
            back_rows[0].append(got[0:2])
            back_rows[1].append(got[2:4])
            back_own.append(got[4:6])
        returns = [
            lax.ppermute(jnp.concatenate(x, axis=0), "rows", perm)
            for x, perm in zip(back_rows, row_perm)
        ] + [jnp.concatenate(back_own, axis=0)]
        last = step == STEPS - 1
        outs = pl.pallas_call(
            functools.partial(update_kernel, 3, last),
            out_shape=[f32_out(6, 2048)] * 2 if last else [f32_out(16, 8, 128), f32_out(6, 2048)] + list_outs,
            in_specs=[VMEM] * 9,
            out_specs=[VMEM] * (2 if last else 5),
            scratch_shapes=[pltpu.VMEM((128, 256 * n), BF16), pltpu.VMEM((256, 256 * n), BF16)],
            compiler_params=params(),
        )(own, recv, field, speed, mass, picks, *returns)
        field, speed = outs[:2]
        outgoing = outs[2:]
    return field, speed


def solution(mesh):
    whole = ("groups", "rows", "cols", "sub")
    in_specs = (
        P(None, whole),
        P(None, whole),
        P(whole),
        P("rows", "cols", ("groups", "sub")),
        P(None, whole),
        P(None, whole),
        P(whole),
        P(whole),
        P(),
    )
    out_specs = (P(None, whole), P(None, whole))
    return jax.shard_map(shards, mesh=mesh, in_specs=in_specs, out_specs=out_specs, check_vma=False)
```
